256 devices in a mesh: ctx: 32 (over z_hi, x, y), head: 8 (over z_lo, core).
Axes of the slice: x: 4, y: 4, z: 8 (z_hi: 2, z_lo: 4; z = z_hi * 4 + z_lo), core: 2. Of those that a mesh axis runs over, the one named last changes fastest.
Arguments:
- queries: bfloat16 [2, 8192, 4096], P(None, 'ctx', 'head'), may hold values from -6 to 6
- keys: bfloat16 [2, 8192, 4096], P(None, 'ctx', 'head'), may hold values from -6 to 6
- values: bfloat16 [2, 8192, 4096], P(None, 'ctx', 'head'), may hold values from -6 to 6
- token_gate: float32 [2, 32, 8192], P(None, 'head', 'ctx'), may hold values from 0.2 to 1
- head_rate: float32 [32], P('head'), may hold values from 2.861023e-07 to 0.001953125
- init_state: float32 [32, 128, 128], P('head'), may hold values from -0.53033006 to 0.53033006
- norm_gain: float32 [4096], P('head'), may hold values from 0.5 to 1.5
- out_proj: bfloat16 [4096, 4096], P('head'), may hold values from -0.09375 to 0.09375
- plan: int32 [2], replicated, may hold values from 0 to 1, each once
Outputs:
- layer_out: bfloat16 [8192, 2, 4096], P(('ctx', 'head'))
The draws below stay inside these ranges and needn't reach their ends.
Inputs may be any that keep to these rules, and one draw needn't show every extreme that they name: `plan`: each sequence appears exactly once.
All inputs are finite; a program needn't handle non-finite values.
Results may differ from the reference program's by a relative error of at most 0.0049.
Values sent between devices are 32-bit elements; how exact they have to be, the bound alone decides.
A program may use at most 64 MiB of HBM per device.

```python
import math
import jax
import jax.numpy as jnp
from jax import lax

D = 4096
HEADS = 32
HS = 128
MB = 64
SEQS = 2
TOKENS = 8192


def level_of(stream_key, dims, cuts, smallest, largest):
    def one(dim, shards_of):
        steps = jax.random.uniform(jax.random.fold_in(jax.random.fold_in(stream_key, 6), dim), (shards_of,), jnp.float32, smallest / len(cuts), largest / len(cuts))
        return jnp.repeat(jnp.exp(steps), dims[dim] // shards_of).reshape((-1,) + (1,) * (len(dims) - dim - 1))

    level = one(*cuts[0])
    for cut in cuts[1:]:
        level = level * one(*cut)
    return level


def normal_values(rng, dims, width, most, cuts=(), held_as=jnp.bfloat16):
    level = level_of(rng, dims, cuts, -0.22, 0.18) if cuts else 1.0
    drawn = jax.random.normal(rng, dims, jnp.float32) * width * level
    return jnp.minimum(jnp.maximum(drawn, -most), most).astype(held_as)


def setup_inputs(seed: int = 0) -> dict:
    arg_keys = jax.random.split(jax.random.key(seed), 10)
    queries = normal_values(arg_keys[0], (SEQS, TOKENS, HEADS * HS), 1.0, 6.0, ((1, 32), (2, 8)))
    keys = normal_values(arg_keys[1], (SEQS, TOKENS, HEADS * HS), 1.0, 6.0, ((1, 32), (2, 8)))
    values = normal_values(arg_keys[2], (SEQS, TOKENS, HEADS * HS), 1.0, 6.0, ((1, 32), (2, 8)))
    token_gate = jnp.clip(0.2 + 0.8 * jax.random.uniform(arg_keys[3], (SEQS, HEADS, TOKENS), jnp.float32) ** level_of(arg_keys[3], (SEQS, HEADS, TOKENS), ((1, 8), (2, 32)), -0.2, 0.2), 0.2, 1.0)
    head_rate = jnp.clip(jnp.exp(math.log(0.001953125) - 8.8285918 * jax.random.uniform(arg_keys[4], (HEADS,), jnp.float32) ** level_of(arg_keys[4], (HEADS,), ((0, 8),), -0.2, 0.2)), 2.8610230629055877e-07, 0.001953125)
    init_state = normal_values(arg_keys[5], (HEADS, HS, HS), (HS ** -0.5), 0.53033006, ((0, 8),), jnp.float32)
    norm_gain = jnp.clip(1.0 + 0.1 * jax.random.normal(arg_keys[6], (HEADS * HS,), jnp.float32), 0.5, 1.5)
    out_proj = normal_values(arg_keys[7], (HEADS * HS, D), (HEADS * HS) ** -0.5, 0.09375, ((0, 8),))
    plan = jax.random.permutation(arg_keys[8], SEQS).astype(jnp.int32)
    return {"queries": queries, "keys": keys, "values": values, "token_gate": token_gate, "head_rate": head_rate, "init_state": init_state, "norm_gain": norm_gain, "out_proj": out_proj, "plan": plan}


EPS = 1e-06

def run_sequence(qs, ks, vs, eta, start):
    best = lax.Precision.HIGHEST
    blocks = TOKENS // MB

    def split(arr):
        arr = arr.astype(jnp.float32).reshape(blocks, MB, HEADS, HS)
        return jnp.transpose(arr, (0, 2, 1, 3))
    qb, kb, vb = (split(qs), split(ks), split(vs))
    eb = jnp.transpose(eta.reshape(HEADS, blocks, MB), (1, 0, 2))
    lower = jnp.arange(MB)[:, None] >= jnp.arange(MB)[None, :]

    def step(weights, blk):
        qm, km, vm, em = blk
        err = jnp.einsum('hmi,hij->hmj', km, weights, precision=best) - vm
        qw = jnp.einsum('hmi,hij->hmj', qm, weights, precision=best)
        scores = jnp.einsum('hmi,hni->hmn', qm, km, precision=best) * em[:, None, :]
        scores = jnp.where(lower[None], scores, 0.0)
        zout = qw - jnp.einsum('hmn,hnj->hmj', scores, err, precision=best)
        weights = weights - jnp.einsum('hmi,hmj->hij', km * em[..., None], err, precision=best)
        return (weights, zout)
    _, zall = lax.scan(step, start, (qb, kb, vb, eb))
    return jnp.transpose(zall, (0, 2, 1, 3)).reshape(TOKENS, HEADS, HS)

def reference(queries, keys, values, token_gate, head_rate, init_state, norm_gain, out_proj, plan):
    gain = norm_gain.reshape(HEADS, HS)
    outputs = []
    for step_index in range(SEQS):
        seq = plan[step_index]
        eta = token_gate[seq] * head_rate[:, None]
        zvals = run_sequence(queries[seq], keys[seq], values[seq], eta, init_state)
        scale = lax.rsqrt(lax.optimization_barrier(jnp.mean(zvals * zvals, axis=-1, keepdims=True)) + EPS)
        normed = (zvals * scale * gain[None]).astype(jnp.bfloat16).reshape(TOKENS, HEADS * HS)
        outputs.append(jnp.dot(normed, out_proj, preferred_element_type=jnp.float32).astype(jnp.bfloat16))
    return jnp.stack(outputs, axis=1)
```

```python
import jax
import jax.numpy as jnp
from jax import lax
from jax.experimental import pallas as pl
from jax.experimental.pallas import tpu as pltpu
from jax.sharding import PartitionSpec as P

HS = 128
MB = 64
EPS = 1e-06
MESH = pl.DeviceIdType.MESH
F32 = jnp.float32
BF16 = jnp.bfloat16
PLANE = 16
SLOTS = 4


def halves(a):
    hi = a.astype(BF16)
    return hi, (a - hi.astype(F32)).astype(BF16)


def mm(a, b):
    return jnp.dot(a, b, preferred_element_type=F32)


def mm3(a, b):
    return mm(a[0], b[0]) + (mm(a[0], b[1]) + mm(a[1], b[0]))


def nt(a, b):
    return lax.dot_general(a, b, (((1,), (1,)), ((), ())), preferred_element_type=F32)


def tn(a, b):
    return lax.dot_general(a, b, (((0,), (0,)), ((), ())), preferred_element_type=F32)


def slice_maps(q, k, v, ecol):
    rows = k.shape[0]
    gram = nt(k, k)
    kv = jnp.concatenate([k, v], axis=1).astype(F32)
    first = halves(kv[:MB] * ecol[:MB])
    his, los = [first[0]], [first[1]]
    for start in range(MB, rows, MB):
        left = halves(gram[start : start + MB, :start])
        hi, lo = jnp.concatenate(his, axis=0), jnp.concatenate(los, axis=0)
        part = kv[start : start + MB] - mm3(left, (hi, lo))
        nxt = halves(part * ecol[start : start + MB])
        his.append(nxt[0])
        los.append(nxt[1])
    hi, lo = jnp.concatenate(his, axis=0), jnp.concatenate(los, axis=0)
    moved = tn(k, hi) + tn(k, lo)
    r = lax.broadcasted_iota(jnp.int32, (HS, HS), 0)
    c = lax.broadcasted_iota(jnp.int32, (HS, HS), 1)
    eye = jnp.where(r == c, 1.0, 0.0).astype(F32)
    fd = jnp.concatenate([eye - moved[:, :HS], moved[:, HS:]], axis=1)
    scores = nt(q, k)
    r = lax.broadcasted_iota(jnp.int32, (rows, rows), 0)
    c = lax.broadcasted_iota(jnp.int32, (rows, rows), 1)
    scores = halves(jnp.where(c <= r, scores, 0.0))
    read = mm3(scores, (hi, lo))
    return fd, q.astype(F32) - read[:, :HS], read[:, HS:]


def local_kernel(q_ref, k_ref, v_ref, gate_ref, rate_ref, fd_ref, qh_ref, ql_ref, z0_ref):
    heads = gate_ref.shape[1]
    rows = gate_ref.shape[2]
    gate = gate_ref[0]
    eta = jnp.concatenate(
        [gate[h : h + 1] * rate_ref[h] for h in range(heads)] + [jnp.zeros((8 - heads, rows), F32)], axis=0
    )
    etat = eta.T
    for h in range(heads):
        cols = slice(h * HS, (h + 1) * HS)
        fd, qt, z0 = slice_maps(q_ref[0, :, cols], k_ref[0, :, cols], v_ref[0, :, cols], etat[:, h : h + 1])
        fd_ref[h] = fd
        hi, lo = halves(qt)
        qh_ref[h] = hi
        ql_ref[h] = lo
        z0_ref[h] = z0


def copy_wait(ref, sem):
    pltpu.make_async_copy(ref, ref, sem).wait()


def scan_kernel(
    fd_ref, init_ref, w_ref, recv, hist, wout, xw, wbuf, fd_send, fd_recv, w_send, w_recv, x_send, x_recv
):
    me_c, me_h = lax.axis_index("ctx"), lax.axis_index("head")
    zhi, p = me_c // PLANE, lax.rem(me_c, PLANE)
    x, y = p // 4, lax.rem(p, 4)
    core = lax.rem(me_h, 2)
    pairs = fd_ref.shape[0]
    heads = init_ref.shape[0]

    barrier = pltpu.get_barrier_semaphore()
    for step in range(1, PLANE):
        other = zhi * PLANE + lax.rem(p + step, PLANE)
        pl.semaphore_signal(barrier, inc=1, device_id=(other, me_h), device_id_type=MESH)
    partner = (1 - zhi) * PLANE + p
    pl.semaphore_signal(barrier, inc=1, device_id=(partner, me_h), device_id_type=MESH)
    pl.semaphore_wait(barrier, PLANE)

    def home(j):
        s, hh = j // heads, j % heads
        return 4 * hh + 2 * core + (hh + s) % 2

    def fd_copy(j):
        return pltpu.make_async_remote_copy(
            src_ref=fd_ref.at[j],
            dst_ref=recv.at[p],
            send_sem=fd_send.at[j],
            recv_sem=fd_recv.at[p],
            device_id=(zhi * PLANE + home(j), me_h),
            device_id_type=MESH,
        )

    for j in range(pairs):
        to = home(j)

        @pl.when(to != p)
        def _():
            fd_copy(j).start()

        @pl.when(to == p)
        def _():
            pltpu.make_async_copy(fd_ref.at[j], recv.at[p], fd_recv.at[p]).start()

    handler = y // 2 == core
    mine = lax.rem(x + y, 2) * heads + x

    def w_copy(c):
        return pltpu.make_async_remote_copy(
            src_ref=wout.at[c],
            dst_ref=wbuf.at[mine],
            send_sem=w_send.at[c],
            recv_sem=w_recv.at[mine],
            device_id=(zhi * PLANE + c, me_h),
            device_id_type=MESH,
        )

    def give(c):
        @pl.when(c != p)
        def _():
            w_copy(c).start()

        @pl.when(c == p)
        def _():
            pltpu.make_async_copy(wout.at[c], wbuf.at[mine], w_recv.at[mine]).start()

    x_copy = pltpu.make_async_remote_copy(
        src_ref=xw.at[0],
        dst_ref=xw.at[1],
        send_sem=x_send,
        recv_sem=x_recv,
        device_id=(PLANE + p, me_h),
        device_id_type=MESH,
    )

    @pl.when(handler)
    def _():
        r = lax.broadcasted_iota(jnp.int32, (HS, HS), 0)
        c = lax.broadcasted_iota(jnp.int32, (HS, HS), 1)
        eye = jnp.where(r == c, 1.0, 0.0).astype(F32)
        first = jnp.where(zhi == 0, 1.0, 0.0).astype(F32)
        start = jnp.concatenate([eye * (1.0 - first), init_ref[x] * first], axis=1)

        def step(c, state):
            copy_wait(recv.at[c], fd_recv.at[c])

            @pl.when(zhi == 0)
            def _():
                wout[c] = state[:, HS:]
                give(c)

            @pl.when(zhi == 1)
            def _():
                hist[c] = state

            fd = recv[c]
            nxt = mm3(halves(fd[:, :HS]), halves(state))
            return nxt + jnp.concatenate([jnp.zeros((HS, HS), F32), fd[:, HS:]], axis=1)

        last = lax.fori_loop(0, PLANE, step, start)

        @pl.when(zhi == 0)
        def _():
            xw[0] = last[:, HS:]
            x_copy.start()

        @pl.when(zhi == 1)
        def _():
            x_copy.wait_recv()
            entry = halves(xw[1])

            def apply(c, carry):
                state = hist[c]
                wout[c] = mm3(halves(state[:, :HS]), entry) + state[:, HS:]
                give(c)
                return carry

            lax.fori_loop(0, PLANE, apply, 0)

    for j in range(pairs):
        copy_wait(wbuf.at[j], w_recv.at[j])
        w_ref[j] = wbuf[j]

    for j in range(pairs):

        @pl.when(home(j) != p)
        def _():
            fd_copy(j).wait_send()

    @pl.when(handler)
    def _():
        def done(c, carry):
            @pl.when(c != p)
            def _():
                w_copy(c).wait_send()

            return carry

        lax.fori_loop(0, PLANE, done, 0)

        @pl.when(zhi == 0)
        def _():
            x_copy.wait_send()


def out_kernel(
    qh_ref, ql_ref, z0_ref, w_ref, gain_ref, proj_ref, out_ref,
    normed, prod, sib, rbuf, lbuf, sib_send, sib_recv, r_send, r_recv, l_send, l_recv,
):
    me_c, me_h = lax.axis_index("ctx"), lax.axis_index("head")
    z, core = me_h // 2, lax.rem(me_h, 2)
    twin = z * 2 + (1 - core)
    seqs, parts = prod.shape[0], prod.shape[1]
    width = prod.shape[-1]
    heads = qh_ref.shape[0] // seqs
    rows = qh_ref.shape[1]

    barrier = pltpu.get_barrier_semaphore()
    pl.semaphore_signal(barrier, inc=1, device_id=(me_c, twin), device_id_type=MESH)

    @pl.when(z > 0)
    def _():
        pl.semaphore_signal(barrier, inc=1, device_id=(me_c, me_h - 2), device_id_type=MESH)

    @pl.when(z < SLOTS - 1)
    def _():
        pl.semaphore_signal(barrier, inc=1, device_id=(me_c, me_h + 2), device_id_type=MESH)

    count = 1 + jnp.where(z > 0, 1, 0) + jnp.where(z < SLOTS - 1, 1, 0)
    pl.semaphore_wait(barrier, count)

    def sib_copy(s, q):
        return pltpu.make_async_remote_copy(
            src_ref=prod.at[s, q, 1 - core],
            dst_ref=sib.at[s, q],
            send_sem=sib_send.at[s, q],
            recv_sem=sib_recv.at[s, q],
            device_id=(me_c, twin),
            device_id_type=MESH,
        )

    def line_copy(s, q, b, step):
        buf, send, recv = (rbuf, r_send, r_recv) if step > 0 else (lbuf, l_send, l_recv)
        return pltpu.make_async_remote_copy(
            src_ref=prod.at[s, q, core, b],
            dst_ref=buf.at[s, q, b],
            send_sem=send.at[s, q, b],
            recv_sem=recv.at[s, q, b],
            device_id=(me_c, me_h + step),
            device_id_type=MESH,
        )

    for s in range(seqs):
        for h in range(heads):
            j = s * heads + h
            cols = slice(h * HS, (h + 1) * HS)
            zval = mm3((qh_ref[j], ql_ref[j]), halves(w_ref[j])) + z0_ref[j]
            scale = lax.rsqrt(jnp.mean(zval * zval, axis=-1, keepdims=True) + EPS)
            normed[s, :, cols] = (zval * scale * gain_ref[:, cols]).astype(BF16)

        def project(q, carry):
            start = pl.multiple_of(q * width, width)
            part = mm(normed[s], proj_ref[:, pl.ds(start, width)])
            part = part.reshape(SLOTS, 2, rows // (2 * SLOTS), width)
            prod[s, q, 0] = part[:, 0]
            prod[s, q, 1] = part[:, 1]
            sib_copy(s, q).start()
            return carry

        lax.fori_loop(0, parts, project, 0)

    def each(body):
        lax.fori_loop(0, seqs * parts, lambda i, carry: (body(i // parts, lax.rem(i, parts)), carry)[1], 0)

    def pair_sum(s, q):
        sib_copy(s, q).wait_recv()
        sib_copy(s, q).wait_send()
        for b in range(SLOTS):
            prod[s, q, core, b] += sib[s, q, b]

        @pl.when(z == 0)
        def _():
            for b in range(SLOTS - 1, 0, -1):
                line_copy(s, q, b, 2).start()

        @pl.when(z == SLOTS - 1)
        def _():
            for b in range(SLOTS - 1):
                line_copy(s, q, b, -2).start()

    each(pair_sum)

    def forward(s, q):
        for b in range(SLOTS - 1, 0, -1):

            @pl.when(jnp.logical_and(z > 0, z < b))
            def _():
                copy_wait(rbuf.at[s, q, b], r_recv.at[s, q, b])
                prod[s, q, core, b] += rbuf[s, q, b]
                line_copy(s, q, b, 2).start()

        for b in range(SLOTS - 1):

            @pl.when(jnp.logical_and(z < SLOTS - 1, z > b))
            def _():
                copy_wait(lbuf.at[s, q, b], l_recv.at[s, q, b])
                prod[s, q, core, b] += lbuf[s, q, b]
                line_copy(s, q, b, -2).start()

    @pl.when(jnp.logical_and(z > 0, z < SLOTS - 1))
    def _():
        each(forward)

    for s in range(seqs):
        for q in range(parts):
            cols = slice(q * width, (q + 1) * width)

            @pl.when(z > 0)
            def _():
                copy_wait(rbuf.at[s, q, z], r_recv.at[s, q, z])
                prod[s, q, core, z] += rbuf[s, q, z]

            @pl.when(z < SLOTS - 1)
            def _():
                copy_wait(lbuf.at[s, q, z], l_recv.at[s, q, z])
                prod[s, q, core, z] += lbuf[s, q, z]

            out_ref[s, :, cols] = prod[s, q, core, z].astype(BF16)

    def finish(s, q):
        for b in range(SLOTS):

            @pl.when(z < b)
            def _():
                line_copy(s, q, b, 2).wait_send()

            @pl.when(z > b)
            def _():
                line_copy(s, q, b, -2).wait_send()

    each(finish)


def per_device(queries, keys, values, token_gate, head_rate, init_state, norm_gain, out_proj, plan):
    seqs, rows, width = queries.shape
    heads = init_state.shape[0]
    pairs = seqs * heads
    model = out_proj.shape[1]
    vmem = pl.BlockSpec(memory_space=pltpu.VMEM)
    token_spec = pl.BlockSpec((1, rows, width), lambda s: (s, 0, 0))

    def pair_spec(a, b):
        return pl.BlockSpec((heads, a, b), lambda s: (s, 0, 0))

    fd, qh, ql, z0 = pl.pallas_call(
        local_kernel,
        grid=(seqs,),
        in_specs=[
            token_spec,
            token_spec,
            token_spec,
            pl.BlockSpec((1, heads, rows), lambda s: (s, 0, 0)),
            pl.BlockSpec(memory_space=pltpu.SMEM),
        ],
        out_specs=[pair_spec(HS, 2 * HS), pair_spec(rows, HS), pair_spec(rows, HS), pair_spec(rows, HS)],
        out_shape=[
            jax.ShapeDtypeStruct((pairs, HS, 2 * HS), F32),
            jax.ShapeDtypeStruct((pairs, rows, HS), BF16),
            jax.ShapeDtypeStruct((pairs, rows, HS), BF16),
            jax.ShapeDtypeStruct((pairs, rows, HS), F32),
        ],
        compiler_params=pltpu.CompilerParams(vmem_limit_bytes=40 * 2**20),
        name="slice_maps",
    )(queries, keys, values, token_gate, head_rate)

    dma = pltpu.SemaphoreType.DMA
    weights = pl.pallas_call(
        scan_kernel,
        out_shape=jax.ShapeDtypeStruct((pairs, HS, HS), F32),
        in_specs=[vmem] * 2,
        out_specs=vmem,
        scratch_shapes=[
            pltpu.VMEM((PLANE, HS, 2 * HS), F32),
            pltpu.VMEM((PLANE, HS, 2 * HS), F32),
            pltpu.VMEM((PLANE, HS, HS), F32),
            pltpu.VMEM((2, HS, HS), F32),
            pltpu.VMEM((pairs, HS, HS), F32),
            dma((pairs,)),
            dma((PLANE,)),
            dma((PLANE,)),
            dma((pairs,)),
            dma,
            dma,
        ],
        compiler_params=pltpu.CompilerParams(
            collective_id=0, has_side_effects=True, vmem_limit_bytes=24 * 2**20
        ),
        name="state_scan",
    )(fd, init_state)

    parts = 4
    cols = model // parts
    share = rows // (2 * SLOTS)
    line = pltpu.VMEM((seqs, parts, SLOTS, share, cols), F32)
    summed = pl.pallas_call(
        out_kernel,
        out_shape=jax.ShapeDtypeStruct((seqs, share, model), BF16),
        in_specs=[vmem] * 6,
        out_specs=vmem,
        scratch_shapes=[
            pltpu.VMEM((seqs, rows, width), BF16),
            pltpu.VMEM((seqs, parts, 2, SLOTS, share, cols), F32),
            line,
            line,
            line,
            dma((seqs, parts)),
            dma((seqs, parts)),
            dma((seqs, parts, SLOTS)),
            dma((seqs, parts, SLOTS)),
            dma((seqs, parts, SLOTS)),
            dma((seqs, parts, SLOTS)),
        ],
        compiler_params=pltpu.CompilerParams(
            collective_id=1, has_side_effects=True, vmem_limit_bytes=48 * 2**20
        ),
        name="project_sum",
    )(qh, ql, z0, weights, norm_gain.reshape(1, width), out_proj)
    straight = plan[0] == 0
    return jnp.stack(
        [jnp.where(straight, summed[0], summed[1]), jnp.where(straight, summed[1], summed[0])], axis=1
    )


def solution(mesh):
    return jax.shard_map(
        per_device,
        mesh=mesh,
        in_specs=(
            P(None, "ctx", "head"),
            P(None, "ctx", "head"),
            P(None, "ctx", "head"),
            P(None, "head", "ctx"),
            P("head"),
            P("head", None, None),
            P("head"),
            P("head", None),
            P(),
        ),
        out_specs=P(("ctx", "head"), None, None),
        check_vma=False,
    )
```

```python
import jax
import jax.numpy as jnp
from jax import lax
from jax.experimental import pallas as pl
from jax.experimental.pallas import tpu as pltpu
from jax.sharding import PartitionSpec as P

HS = 128
MB = 64
EPS = 1e-06
MESH = pl.DeviceIdType.MESH
F32 = jnp.float32
BF16 = jnp.bfloat16
PLANE = 16
SLOTS = 4


def halves(a):
    hi = a.astype(BF16)
    return hi, (a - hi.astype(F32)).astype(BF16)


def mm(a, b):
    return jnp.dot(a, b, preferred_element_type=F32)


def mm3(a, b):
    return mm(a[0], b[0]) + (mm(a[0], b[1]) + mm(a[1], b[0]))


def nt(a, b):
    return lax.dot_general(a, b, (((1,), (1,)), ((), ())), preferred_element_type=F32)


def tn(a, b):
    return lax.dot_general(a, b, (((0,), (0,)), ((), ())), preferred_element_type=F32)


def spread(k, v, ecol):
    rows = k.shape[0]
    gram = nt(k, k)
    kv = jnp.concatenate([k, v], axis=1).astype(F32)
    first = halves(kv[:MB] * ecol[:MB])
    his, los = [first[0]], [first[1]]
    for start in range(MB, rows, MB):
        left = halves(gram[start : start + MB, :start])
        hi, lo = jnp.concatenate(his, axis=0), jnp.concatenate(los, axis=0)
        part = kv[start : start + MB] - mm3(left, (hi, lo))
        nxt = halves(part * ecol[start : start + MB])
        his.append(nxt[0])
        los.append(nxt[1])
    return jnp.concatenate(his, axis=0), jnp.concatenate(los, axis=0)


def slice_map(k, hi, lo):
    moved = tn(k, hi) + tn(k, lo)
    r = lax.broadcasted_iota(jnp.int32, (HS, HS), 0)
    c = lax.broadcasted_iota(jnp.int32, (HS, HS), 1)
    eye = jnp.where(r == c, 1.0, 0.0).astype(F32)
    return jnp.concatenate([eye - moved[:, :HS], moved[:, HS:]], axis=1)


def readout(q, k, hi, lo):
    rows = q.shape[0]
    scores = nt(q, k)
    r = lax.broadcasted_iota(jnp.int32, (rows, rows), 0)
    c = lax.broadcasted_iota(jnp.int32, (rows, rows), 1)
    scores = halves(jnp.where(c <= r, scores, 0.0))
    read = mm3(scores, (hi, lo))
    return q.astype(F32) - read[:, :HS], read[:, HS:]


def after(earlier, later):
    moved = mm3(halves(later[:, :HS]), halves(earlier))
    return moved + jnp.concatenate([jnp.zeros((HS, HS), F32), later[:, HS:]], axis=1)


def applied(change, state):
    return mm3(halves(change[:, :HS]), halves(state)) + change[:, HS:]


def copy_wait(ref, sem):
    pltpu.make_async_copy(ref, ref, sem).wait()


def layer_kernel(
    q_hbm, k_hbm, v_hbm, gate_hbm, rate_hbm, init_hbm, gain_hbm, proj_hbm, out_ref,
    q_ref, k_ref, v_ref, gate_ref, rate_ref, init_ref, gain_ref, proj_ref,
    ehi, elo, fd_ref, qh_ref, ql_ref, z0_ref,
    recv, total, enter, wout, xw, wbuf, normed, prod, sib, rbuf, lbuf,
    in_sem, fd_send, fd_recv, w_send, w_recv, x_send, x_recv,
    sib_send, sib_recv, r_send, r_recv, l_send, l_recv,
):
    me_c, me_h = lax.axis_index("ctx"), lax.axis_index("head")
    zhi, p = me_c // PLANE, lax.rem(me_c, PLANE)
    x, y = p // 4, lax.rem(p, 4)
    z, core = me_h // 2, lax.rem(me_h, 2)
    twin = z * 2 + (1 - core)
    seqs, rows = q_ref.shape[0], q_ref.shape[1]
    heads = init_ref.shape[0]
    pairs = seqs * heads
    parts, width = prod.shape[1], prod.shape[-1]

    loads = []
    order = [(k_hbm.at[0], k_ref.at[0]), (v_hbm.at[0], v_ref.at[0]), (gate_hbm, gate_ref), (rate_hbm, rate_ref)]
    order += [(k_hbm.at[1], k_ref.at[1]), (v_hbm.at[1], v_ref.at[1]), (q_hbm, q_ref), (init_hbm, init_ref)]
    order += [(gain_hbm, gain_ref), (proj_hbm, proj_ref)]
    for i, (src, dst) in enumerate(order):
        loads.append(pltpu.make_async_copy(src, dst, in_sem.at[i]))
        loads[-1].start()

    barrier = pltpu.get_barrier_semaphore()
    for step in range(1, PLANE):
        other = zhi * PLANE + lax.rem(p + step, PLANE)
        pl.semaphore_signal(barrier, inc=1, device_id=(other, me_h), device_id_type=MESH)
    partner = (1 - zhi) * PLANE + p
    pl.semaphore_signal(barrier, inc=1, device_id=(partner, me_h), device_id_type=MESH)
    pl.semaphore_signal(barrier, inc=1, device_id=(me_c, twin), device_id_type=MESH)

    @pl.when(z > 0)
    def _():
        pl.semaphore_signal(barrier, inc=1, device_id=(me_c, me_h - 2), device_id_type=MESH)

    @pl.when(z < SLOTS - 1)
    def _():
        pl.semaphore_signal(barrier, inc=1, device_id=(me_c, me_h + 2), device_id_type=MESH)

    for i in range(4):
        loads[i].wait()
    etas = []
    for s in range(seqs):
        eta = [gate_ref[s, h : h + 1] * rate_ref[0:1, h : h + 1] for h in range(heads)]
        etas.append(jnp.concatenate(eta + [jnp.zeros((8 - heads, rows), F32)], axis=0).T)

    def home(s, h):
        return 4 * h + 2 * core + lax.rem(h + s, 2)

    def fd_copy(s, h):
        return pltpu.make_async_remote_copy(
            src_ref=fd_ref.at[s * heads + h],
            dst_ref=recv.at[p],
            send_sem=fd_send.at[s * heads + h],
            recv_sem=fd_recv.at[p],
            device_id=(zhi * PLANE + home(s, h), me_h),
            device_id_type=MESH,
        )

    for s in range(seqs):
        if s == 1:
            loads[4].wait()
            loads[5].wait()
        for h in range(heads):
            cols = slice(h * HS, (h + 1) * HS)
            k = k_ref[s, :, cols]
            hi, lo = spread(k, v_ref[s, :, cols], etas[s][:, h : h + 1])
            ehi[s * heads + h] = hi
            elo[s * heads + h] = lo
            fd_ref[s * heads + h] = slice_map(k, hi, lo)
        if s == 0:
            count = 2 + PLANE - 1 + jnp.where(z > 0, 1, 0) + jnp.where(z < SLOTS - 1, 1, 0)
            pl.semaphore_wait(barrier, count)
        for i in range(heads):
            h = lax.rem(x + i, heads)
            to = home(s, h)

            @pl.when(to != p)
            def _():
                fd_copy(s, h).start()

            @pl.when(to == p)
            def _():
                pltpu.make_async_copy(fd_ref.at[s * heads + h], recv.at[p], fd_recv.at[p]).start()

    loads[6].wait()
    for j in range(pairs):
        s, h = j // heads, j % heads
        cols = slice(h * HS, (h + 1) * HS)
        qt, z0 = readout(q_ref[s, :, cols], k_ref[s, :, cols], ehi[j], elo[j])
        hi, lo = halves(qt)
        qh_ref[j] = hi
        ql_ref[j] = lo
        z0_ref[j] = z0
    for load in loads[7:]:
        load.wait()

    handler = y // 2 == core
    mine = lax.rem(x + y, 2) * heads + x

    def w_copy(c):
        return pltpu.make_async_remote_copy(
            src_ref=wout.at[c],
            dst_ref=wbuf.at[mine],
            send_sem=w_send.at[c],
            recv_sem=w_recv.at[mine],
            device_id=(zhi * PLANE + c, me_h),
            device_id_type=MESH,
        )

    x_copy = pltpu.make_async_remote_copy(
        src_ref=xw.at[0],
        dst_ref=xw.at[1],
        send_sem=x_send,
        recv_sem=x_recv,
        device_id=(PLANE + p, me_h),
        device_id_type=MESH,
    )

    @pl.when(handler)
    def _():
        for i in range(4):
            for g in range(4):
                c = 4 * g + i
                copy_wait(recv.at[c], fd_recv.at[c])
                if i > 0:
                    recv[c] = after(recv[c - 1], recv[c])
        total[0] = recv[3]
        for g in range(1, 4):
            total[g] = after(total[g - 1], recv[4 * g + 3])

        @pl.when(zhi == 0)
        def _():
            enter[0] = init_ref[x]
            xw[0] = applied(total[3], init_ref[x])
            x_copy.start()

        @pl.when(zhi == 1)
        def _():
            x_copy.wait_recv()
            enter[0] = xw[1]

        for g in range(1, 4):
            enter[g] = applied(total[g - 1], enter[0])
        for i in range(4):
            g = lax.rem(x + i, 4)
            wout[4 * g] = enter[g]
            for k in range(1, 4):
                wout[4 * g + k] = applied(recv[4 * g + k - 1], enter[g])
            for k in range(4):
                c = 4 * g + k

                @pl.when(c != p)
                def _():
                    w_copy(c).start()

                @pl.when(c == p)
                def _():
                    pltpu.make_async_copy(wout.at[c], wbuf.at[mine], w_recv.at[mine]).start()

    def sib_copy(s, q):
        return pltpu.make_async_remote_copy(
            src_ref=prod.at[s, q, 1 - core],
            dst_ref=sib.at[s, q],
            send_sem=sib_send.at[s, q],
            recv_sem=sib_recv.at[s, q],
            device_id=(me_c, twin),
            device_id_type=MESH,
        )

    def line_copy(s, q, b, step):
        buf, send, got = (rbuf, r_send, r_recv) if step > 0 else (lbuf, l_send, l_recv)
        return pltpu.make_async_remote_copy(
            src_ref=prod.at[s, q, core, b],
            dst_ref=buf.at[s, q, b],
            send_sem=send.at[s, q, b],
            recv_sem=got.at[s, q, b],
            device_id=(me_c, me_h + step),
            device_id_type=MESH,
        )

    def each(body):
        lax.fori_loop(0, parts, lambda q, carry: (body(q), carry)[1], 0)

    def outputs(s):
        for h in range(heads):
            j = s * heads + h
            cols = slice(h * HS, (h + 1) * HS)
            copy_wait(wbuf.at[j], w_recv.at[j])
            zval = mm3((qh_ref[j], ql_ref[j]), halves(wbuf[j])) + z0_ref[j]
            scale = lax.rsqrt(jnp.mean(zval * zval, axis=-1, keepdims=True) + EPS)
            normed[s, :, cols] = (zval * scale * gain_ref[:, cols]).astype(BF16)

        def project(q):
            start = pl.multiple_of(q * width, width)
            part = mm(normed[s], proj_ref[:, pl.ds(start, width)])
            part = part.reshape(SLOTS, 2, rows // (2 * SLOTS), width)
            prod[s, q, 0] = part[:, 0]
            prod[s, q, 1] = part[:, 1]
            sib_copy(s, q).start()

        each(project)

    def pair_sums(s):
        def pair_sum(q):
            sib_copy(s, q).wait_recv()
            sib_copy(s, q).wait_send()
            for b in range(SLOTS):
                prod[s, q, core, b] += sib[s, q, b]

            @pl.when(z == 0)
            def _():
                for b in range(SLOTS - 1, 0, -1):
                    line_copy(s, q, b, 2).start()

            @pl.when(z == SLOTS - 1)
            def _():
                for b in range(SLOTS - 1):
                    line_copy(s, q, b, -2).start()

        each(pair_sum)

    def forwards(s):
        def forward(q):
            for b in range(SLOTS - 1, 0, -1):

                @pl.when(jnp.logical_and(z > 0, z < b))
                def _():
                    copy_wait(rbuf.at[s, q, b], r_recv.at[s, q, b])
                    prod[s, q, core, b] += rbuf[s, q, b]
                    line_copy(s, q, b, 2).start()

            for b in range(SLOTS - 1):

                @pl.when(jnp.logical_and(z < SLOTS - 1, z > b))
                def _():
                    copy_wait(lbuf.at[s, q, b], l_recv.at[s, q, b])
                    prod[s, q, core, b] += lbuf[s, q, b]
                    line_copy(s, q, b, -2).start()

        @pl.when(jnp.logical_and(z > 0, z < SLOTS - 1))
        def _():
            each(forward)

    outputs(0)
    pair_sums(0)
    outputs(1)
    forwards(0)
    pair_sums(1)
    forwards(1)

    for s in range(seqs):
        for q in range(parts):
            cols = slice(q * width, (q + 1) * width)

            @pl.when(z > 0)
            def _():
                copy_wait(rbuf.at[s, q, z], r_recv.at[s, q, z])
                prod[s, q, core, z] += rbuf[s, q, z]

            @pl.when(z < SLOTS - 1)
            def _():
                copy_wait(lbuf.at[s, q, z], l_recv.at[s, q, z])
                prod[s, q, core, z] += lbuf[s, q, z]

            out_ref[s, :, cols] = prod[s, q, core, z].astype(BF16)

    def finish(i, carry):
        s, q = i // parts, lax.rem(i, parts)
        for b in range(SLOTS):

            @pl.when(z < b)
            def _():
                line_copy(s, q, b, 2).wait_send()

            @pl.when(z > b)
            def _():
                line_copy(s, q, b, -2).wait_send()

        return carry

    lax.fori_loop(0, seqs * parts, finish, 0)
    for j in range(pairs):

        @pl.when(home(j // heads, j % heads) != p)
        def _():
            fd_copy(j // heads, j % heads).wait_send()

    @pl.when(handler)
    def _():
        def done(c, carry):
            @pl.when(c != p)
            def _():
                w_copy(c).wait_send()

            return carry

        lax.fori_loop(0, PLANE, done, 0)

        @pl.when(zhi == 0)
        def _():
            x_copy.wait_send()


def per_device(queries, keys, values, token_gate, head_rate, init_state, norm_gain, out_proj, plan):
    seqs, rows, width = queries.shape
    heads = init_state.shape[0]
    pairs = seqs * heads
    model = out_proj.shape[1]
    parts = 4
    cols = model // parts
    share = rows // (2 * SLOTS)
    dma = pltpu.SemaphoreType.DMA
    tokens = pltpu.VMEM((seqs, rows, width), BF16)
    line = pltpu.VMEM((seqs, parts, SLOTS, share, cols), F32)
    square = (HS, HS)
    summed = pl.pallas_call(
        layer_kernel,
        out_shape=jax.ShapeDtypeStruct((seqs, share, model), BF16),
        in_specs=[pl.BlockSpec(memory_space=pltpu.HBM)] * 8,
        out_specs=pl.BlockSpec(memory_space=pltpu.VMEM),
        scratch_shapes=[
            tokens,
            tokens,
            tokens,
            pltpu.VMEM((seqs, heads, rows), F32),
            pltpu.VMEM((1, heads), F32),
            pltpu.VMEM((heads,) + square, F32),
            pltpu.VMEM((1, width), F32),
            pltpu.VMEM((width, model), BF16),
            pltpu.VMEM((pairs, rows, 2 * HS), BF16),
            pltpu.VMEM((pairs, rows, 2 * HS), BF16),
            pltpu.VMEM((pairs, HS, 2 * HS), F32),
            pltpu.VMEM((pairs, rows, HS), BF16),
            pltpu.VMEM((pairs, rows, HS), BF16),
            pltpu.VMEM((pairs, rows, HS), F32),
            pltpu.VMEM((PLANE, HS, 2 * HS), F32),
            pltpu.VMEM((4, HS, 2 * HS), F32),
            pltpu.VMEM((4,) + square, F32),
            pltpu.VMEM((PLANE,) + square, F32),
            pltpu.VMEM((2,) + square, F32),
            pltpu.VMEM((pairs,) + square, F32),
            tokens,
            pltpu.VMEM((seqs, parts, 2, SLOTS, share, cols), F32),
            line,
            line,
            line,
            dma((10,)),
            dma((pairs,)),
            dma((PLANE,)),
            dma((PLANE,)),
            dma((pairs,)),
            dma,
            dma,
            dma((seqs, parts)),
            dma((seqs, parts)),
            dma((seqs, parts, SLOTS)),
            dma((seqs, parts, SLOTS)),
            dma((seqs, parts, SLOTS)),
            dma((seqs, parts, SLOTS)),
        ],
        compiler_params=pltpu.CompilerParams(
            collective_id=0, has_side_effects=True, vmem_limit_bytes=56 * 2**20
        ),
        name="layer",
    )(
        queries,
        keys,
        values,
        token_gate,
        head_rate.reshape(1, heads),
        init_state,
        norm_gain.reshape(1, width),
        out_proj,
    )
    straight = plan[0] == 0
    return jnp.stack(
        [jnp.where(straight, summed[0], summed[1]), jnp.where(straight, summed[1], summed[0])], axis=1
    )


def solution(mesh):
    return jax.shard_map(
        per_device,
        mesh=mesh,
        in_specs=(
            P(None, "ctx", "head"),
            P(None, "ctx", "head"),
            P(None, "ctx", "head"),
            P(None, "head", "ctx"),
            P("head"),
            P("head", None, None),
            P("head"),
            P("head", None),
            P(),
        ),
        out_specs=P(("ctx", "head"), None, None),
        check_vma=False,
    )
```

```python
import jax
import jax.numpy as jnp
from jax import lax
from jax.experimental import pallas as pl
from jax.experimental.pallas import tpu as pltpu
from jax.sharding import PartitionSpec as P

HS = 128
MB = 64
EPS = 1e-06
MESH = pl.DeviceIdType.MESH
F32 = jnp.float32
BF16 = jnp.bfloat16
PLANE = 16
SLOTS = 4


def halves(a):
    hi = a.astype(BF16)
    return hi, (a - hi.astype(F32)).astype(BF16)


def mm(a, b):
    return jnp.dot(a, b, preferred_element_type=F32)


def mm3(a, b):
    return mm(a[0], b[0]) + (mm(a[0], b[1]) + mm(a[1], b[0]))


def nt(a, b):
    return lax.dot_general(a, b, (((1,), (1,)), ((), ())), preferred_element_type=F32)


def tn(a, b):
    return lax.dot_general(a, b, (((0,), (0,)), ((), ())), preferred_element_type=F32)


def spread(k, v, ecol):
    rows = k.shape[0]
    gram = nt(k, k)
    kv = jnp.concatenate([k, v], axis=1).astype(F32)
    first = halves(kv[:MB] * ecol[:MB])
    his, los = [first[0]], [first[1]]
    for start in range(MB, rows, MB):
        left = halves(gram[start : start + MB, :start])
        hi, lo = jnp.concatenate(his, axis=0), jnp.concatenate(los, axis=0)
        part = kv[start : start + MB] - mm3(left, (hi, lo))
        nxt = halves(part * ecol[start : start + MB])
        his.append(nxt[0])
        los.append(nxt[1])
    return jnp.concatenate(his, axis=0), jnp.concatenate(los, axis=0)


def slice_map(k, hi, lo):
    moved = tn(k, hi) + tn(k, lo)
    r = lax.broadcasted_iota(jnp.int32, (HS, HS), 0)
    c = lax.broadcasted_iota(jnp.int32, (HS, HS), 1)
    eye = jnp.where(r == c, 1.0, 0.0).astype(F32)
    return jnp.concatenate([eye - moved[:, :HS], moved[:, HS:]], axis=1)


def readout(q, k, hi, lo):
    rows = q.shape[0]
    scores = nt(q, k)
    r = lax.broadcasted_iota(jnp.int32, (rows, rows), 0)
    c = lax.broadcasted_iota(jnp.int32, (rows, rows), 1)
    scores = halves(jnp.where(c <= r, scores, 0.0))
    read = mm3(scores, (hi, lo))
    return q.astype(F32) - read[:, :HS], read[:, HS:]


def after(earlier, later):
    moved = mm3(halves(later[:, :HS]), halves(earlier))
    return moved + jnp.concatenate([jnp.zeros((HS, HS), F32), later[:, HS:]], axis=1)


def applied(change, state):
    return mm3(halves(change[:, :HS]), halves(state)) + change[:, HS:]


def copy_wait(ref, sem):
    pltpu.make_async_copy(ref, ref, sem).wait()


def layer_kernel(
    q_hbm, k_hbm, v_hbm, gate_hbm, rate_hbm, init_hbm, gain_hbm, proj_hbm, out_ref,
    q_ref, k_ref, v_ref, gate_ref, rate_ref, init_ref, gain_ref, proj_ref,
    ehi, elo, fd_ref, qh_ref, ql_ref, z0_ref,
    recv, total, enter, wout, xw, wbuf, normed, prod, sib, rbuf, lbuf, nout, nin, eprod, esib,
    in_sem, fd_send, fd_recv, w_send, w_recv, x_send, x_recv,
    sib_send, sib_recv, r_send, r_recv, l_send, l_recv, n_send, n_recv, e_send, e_recv,
):
    me_c, me_h = lax.axis_index("ctx"), lax.axis_index("head")
    zhi, p = me_c // PLANE, lax.rem(me_c, PLANE)
    x, y = p // 4, lax.rem(p, 4)
    z, core = me_h // 2, lax.rem(me_h, 2)
    twin = z * 2 + (1 - core)
    partner = (1 - zhi) * PLANE + p
    low, high = z == 0, z == SLOTS - 1
    end = jnp.logical_or(low, high)
    far = SLOTS - 1 - z
    left = (jnp.where(low, partner, me_c), jnp.where(low, 2 * (SLOTS - 1) + core, me_h - 2))
    right = (jnp.where(high, partner, me_c), jnp.where(high, core, me_h + 2))
    seqs, rows = q_ref.shape[0], q_ref.shape[1]
    heads = init_ref.shape[0]
    pairs = seqs * heads
    parts, width = prod.shape[1], prod.shape[-1]

    loads = []
    order = [(k_hbm.at[0], k_ref.at[0]), (v_hbm.at[0], v_ref.at[0]), (gate_hbm, gate_ref), (rate_hbm, rate_ref)]
    order += [(k_hbm.at[1], k_ref.at[1]), (v_hbm.at[1], v_ref.at[1]), (q_hbm, q_ref), (init_hbm, init_ref)]
    order += [(gain_hbm, gain_ref), (proj_hbm, proj_ref)]
    for i, (src, dst) in enumerate(order):
        loads.append(pltpu.make_async_copy(src, dst, in_sem.at[i]))
        loads[-1].start()

    barrier = pltpu.get_barrier_semaphore()
    for step in range(1, PLANE):
        other = zhi * PLANE + lax.rem(p + step, PLANE)
        pl.semaphore_signal(barrier, inc=1, device_id=(other, me_h), device_id_type=MESH)
    for other in ((partner, me_h), (me_c, twin), left, right):
        pl.semaphore_signal(barrier, inc=1, device_id=other, device_id_type=MESH)

    for i in range(4):
        loads[i].wait()
    etas = []
    for s in range(seqs):
        eta = [gate_ref[s, h : h + 1] * rate_ref[0:1, h : h + 1] for h in range(heads)]
        etas.append(jnp.concatenate(eta + [jnp.zeros((8 - heads, rows), F32)], axis=0).T)

    def home(s, h):
        return 4 * h + 2 * core + lax.rem(h + s, 2)

    def fd_copy(s, h):
        return pltpu.make_async_remote_copy(
            src_ref=fd_ref.at[s * heads + h],
            dst_ref=recv.at[p],
            send_sem=fd_send.at[s * heads + h],
            recv_sem=fd_recv.at[p],
            device_id=(zhi * PLANE + home(s, h), me_h),
            device_id_type=MESH,
        )

    def send_maps(s):
        for h in range(heads):
            cols = slice(h * HS, (h + 1) * HS)
            k = k_ref[s, :, cols]
            hi, lo = spread(k, v_ref[s, :, cols], etas[s][:, h : h + 1])
            ehi[s * heads + h] = hi
            elo[s * heads + h] = lo
            fd_ref[s * heads + h] = slice_map(k, hi, lo)
        if s == 0:
            pl.semaphore_wait(barrier, PLANE - 1 + 4)
        for i in range(heads):
            h = lax.rem(x + i, heads)
            to = home(s, h)

            @pl.when(to != p)
            def _():
                fd_copy(s, h).start()

            @pl.when(to == p)
            def _():
                pltpu.make_async_copy(fd_ref.at[s * heads + h], recv.at[p], fd_recv.at[p]).start()

    def readouts(s):
        for h in range(heads):
            j = s * heads + h
            cols = slice(h * HS, (h + 1) * HS)
            qt, z0 = readout(q_ref[s, :, cols], k_ref[s, :, cols], ehi[j], elo[j])
            hi, lo = halves(qt)
            qh_ref[j] = hi
            ql_ref[j] = lo
            z0_ref[j] = z0

    send_maps(0)
    loads[6].wait()
    readouts(0)
    loads[4].wait()
    loads[5].wait()
    send_maps(1)
    readouts(1)
    for load in loads[7:]:
        load.wait()

    handler = y // 2 == core
    mine = lax.rem(x + y, 2) * heads + x

    def w_copy(c):
        return pltpu.make_async_remote_copy(
            src_ref=wout.at[c],
            dst_ref=wbuf.at[mine],
            send_sem=w_send.at[c],
            recv_sem=w_recv.at[mine],
            device_id=(zhi * PLANE + c, me_h),
            device_id_type=MESH,
        )

    x_copy = pltpu.make_async_remote_copy(
        src_ref=xw.at[0],
        dst_ref=xw.at[1],
        send_sem=x_send,
        recv_sem=x_recv,
        device_id=(PLANE + p, me_h),
        device_id_type=MESH,
    )

    @pl.when(handler)
    def _():
        for i in range(4):
            for g in range(4):
                c = 4 * g + i
                copy_wait(recv.at[c], fd_recv.at[c])
                if i > 0:
                    recv[c] = after(recv[c - 1], recv[c])
        total[0] = recv[3]
        for g in range(1, 4):
            total[g] = after(total[g - 1], recv[4 * g + 3])

        @pl.when(zhi == 0)
        def _():
            enter[0] = init_ref[x]
            xw[0] = applied(total[3], init_ref[x])
            x_copy.start()

        @pl.when(zhi == 1)
        def _():
            x_copy.wait_recv()
            enter[0] = xw[1]

        for g in range(1, 4):
            enter[g] = applied(total[g - 1], enter[0])
        for i in range(4):
            g = lax.rem(x + i, 4)
            wout[4 * g] = enter[g]
            for k in range(1, 4):
                wout[4 * g + k] = applied(recv[4 * g + k - 1], enter[g])
            for k in range(4):
                c = 4 * g + k

                @pl.when(c != p)
                def _():
                    w_copy(c).start()

                @pl.when(c == p)
                def _():
                    pltpu.make_async_copy(wout.at[c], wbuf.at[mine], w_recv.at[mine]).start()

    def sib_copy(s, q):
        return pltpu.make_async_remote_copy(
            src_ref=prod.at[s, q, 1 - core],
            dst_ref=sib.at[s, q],
            send_sem=sib_send.at[s, q],
            recv_sem=sib_recv.at[s, q],
            device_id=(me_c, twin),
            device_id_type=MESH,
        )

    def line_copy(s, q, b, src, toward_right):
        buf, send, got = (rbuf, r_send, r_recv) if toward_right else (lbuf, l_send, l_recv)
        return pltpu.make_async_remote_copy(
            src_ref=src,
            dst_ref=buf.at[s, q, b],
            send_sem=send.at[s, q, b],
            recv_sem=got.at[s, q, b],
            device_id=right if toward_right else left,
            device_id_type=MESH,
        )

    def own_copy(s, q, b, toward_right):
        return line_copy(s, q, b, prod.at[s, q, core, b], toward_right)

    def far_copy(s, q, toward_right):
        return line_copy(s, q, far, eprod.at[s, q, core], toward_right)

    def rows_copy(s):
        return pltpu.make_async_remote_copy(
            src_ref=nout.at[s],
            dst_ref=nin.at[s],
            send_sem=n_send.at[s],
            recv_sem=n_recv.at[s],
            device_id=(partner, me_h),
            device_id_type=MESH,
        )

    def twin_copy(s, q):
        return pltpu.make_async_remote_copy(
            src_ref=eprod.at[s, q, 1 - core],
            dst_ref=esib.at[s, q],
            send_sem=e_send.at[s, q],
            recv_sem=e_recv.at[s, q],
            device_id=(me_c, twin),
            device_id_type=MESH,
        )

    def each(body):
        lax.fori_loop(0, parts, lambda q, carry: (body(q), carry)[1], 0)

    block = rows // SLOTS
    half = block // 2

    def outputs(s):
        for h in range(heads):
            j = s * heads + h
            cols = slice(h * HS, (h + 1) * HS)
            copy_wait(wbuf.at[j], w_recv.at[j])
            zval = mm3((qh_ref[j], ql_ref[j]), halves(wbuf[j])) + z0_ref[j]
            scale = lax.rsqrt(jnp.mean(zval * zval, axis=-1, keepdims=True) + EPS)
            normed[s, :, cols] = (zval * scale * gain_ref[:, cols]).astype(BF16)

        @pl.when(end)
        def _():
            start = pl.multiple_of(far * block, block)
            nout[s] = normed[s, pl.ds(start, block), :].astype(F32)
            rows_copy(s).start()

        def project(q):
            start = pl.multiple_of(q * width, width)
            part = mm(normed[s], proj_ref[:, pl.ds(start, width)])
            part = part.reshape(SLOTS, 2, half, width)
            prod[s, q, 0] = part[:, 0]
            prod[s, q, 1] = part[:, 1]
            sib_copy(s, q).start()

        each(project)

    def pair_sums(s):
        def pair_sum(q):
            sib_copy(s, q).wait_recv()
            sib_copy(s, q).wait_send()
            for b in range(SLOTS):
                prod[s, q, core, b] += sib[s, q, b]

            @pl.when(z == 0)
            def _():
                own_copy(s, q, 2, True).start()
                own_copy(s, q, 1, True).start()

            @pl.when(z == 1)
            def _():
                own_copy(s, q, 3, True).start()

            @pl.when(z == 2)
            def _():
                own_copy(s, q, 0, False).start()

            @pl.when(z == 3)
            def _():
                own_copy(s, q, 1, False).start()
                own_copy(s, q, 2, False).start()

        each(pair_sum)

    def far_rows(s):
        @pl.when(end)
        def _():
            copy_wait(nin.at[s], n_recv.at[s])
            there = nin[s].astype(BF16)

            def project(q):
                start = pl.multiple_of(q * width, width)
                part = mm(there, proj_ref[:, pl.ds(start, width)])
                eprod[s, q] = part.reshape(2, half, width)
                twin_copy(s, q).start()

            each(project)

            def pair_sum(q):
                twin_copy(s, q).wait_recv()
                eprod[s, q, core] += esib[s, q]

                @pl.when(low)
                def _():
                    far_copy(s, q, False).start()

                @pl.when(high)
                def _():
                    far_copy(s, q, True).start()

            each(pair_sum)

    def take(s, q, b, buf, got):
        copy_wait(buf.at[s, q, b], got.at[s, q, b])
        prod[s, q, core, b] += buf[s, q, b]

    def forwards(s):
        def up(q):
            take(s, q, 2, rbuf, r_recv)
            own_copy(s, q, 2, True).start()
            take(s, q, 0, lbuf, l_recv)
            own_copy(s, q, 0, False).start()

        def down(q):
            take(s, q, 1, lbuf, l_recv)
            own_copy(s, q, 1, False).start()
            take(s, q, 3, rbuf, r_recv)
            own_copy(s, q, 3, True).start()

        @pl.when(z == 1)
        def _():
            each(up)

        @pl.when(z == 2)
        def _():
            each(down)

    outputs(0)
    pair_sums(0)
    far_rows(0)
    outputs(1)
    forwards(0)
    pair_sums(1)
    far_rows(1)
    forwards(1)

    for s in range(seqs):
        for q in range(parts):
            take(s, q, z, rbuf, r_recv)
            take(s, q, z, lbuf, l_recv)
            out_ref[s, :, q * width : (q + 1) * width] = prod[s, q, core, z].astype(BF16)

    def finish(i, carry):
        s, q = i // parts, lax.rem(i, parts)

        @pl.when(z == 0)
        def _():
            own_copy(s, q, 2, True).wait_send()
            own_copy(s, q, 1, True).wait_send()
            far_copy(s, q, False).wait_send()

        @pl.when(z == 1)
        def _():
            own_copy(s, q, 3, True).wait_send()
            own_copy(s, q, 2, True).wait_send()
            own_copy(s, q, 0, False).wait_send()

        @pl.when(z == 2)
        def _():
            own_copy(s, q, 0, False).wait_send()
            own_copy(s, q, 1, False).wait_send()
            own_copy(s, q, 3, True).wait_send()

        @pl.when(z == 3)
        def _():
            own_copy(s, q, 1, False).wait_send()
            own_copy(s, q, 2, False).wait_send()
            far_copy(s, q, True).wait_send()

        @pl.when(end)
        def _():
            twin_copy(s, q).wait_send()

        return carry

    lax.fori_loop(0, seqs * parts, finish, 0)

    @pl.when(end)
    def _():
        for s in range(seqs):
            rows_copy(s).wait_send()

    for j in range(pairs):

        @pl.when(home(j // heads, j % heads) != p)
        def _():
            fd_copy(j // heads, j % heads).wait_send()

    @pl.when(handler)
    def _():
        def done(c, carry):
            @pl.when(c != p)
            def _():
                w_copy(c).wait_send()

            return carry

        lax.fori_loop(0, PLANE, done, 0)

        @pl.when(zhi == 0)
        def _():
            x_copy.wait_send()


def per_device(queries, keys, values, token_gate, head_rate, init_state, norm_gain, out_proj, plan):
    seqs, rows, width = queries.shape
    heads = init_state.shape[0]
    pairs = seqs * heads
    model = out_proj.shape[1]
    parts = 4
    cols = model // parts
    share = rows // (2 * SLOTS)
    dma = pltpu.SemaphoreType.DMA
    tokens = pltpu.VMEM((seqs, rows, width), BF16)
    line = pltpu.VMEM((seqs, parts, SLOTS, share, cols), F32)
    square = (HS, HS)
    summed = pl.pallas_call(
        layer_kernel,
        out_shape=jax.ShapeDtypeStruct((seqs, share, model), BF16),
        in_specs=[pl.BlockSpec(memory_space=pltpu.HBM)] * 8,
        out_specs=pl.BlockSpec(memory_space=pltpu.VMEM),
        scratch_shapes=[
            tokens,
            tokens,
            tokens,
            pltpu.VMEM((seqs, heads, rows), F32),
            pltpu.VMEM((1, heads), F32),
            pltpu.VMEM((heads,) + square, F32),
            pltpu.VMEM((1, width), F32),
            pltpu.VMEM((width, model), BF16),
            pltpu.VMEM((pairs, rows, 2 * HS), BF16),
            pltpu.VMEM((pairs, rows, 2 * HS), BF16),
            pltpu.VMEM((pairs, HS, 2 * HS), F32),
            pltpu.VMEM((pairs, rows, HS), BF16),
            pltpu.VMEM((pairs, rows, HS), BF16),
            pltpu.VMEM((pairs, rows, HS), F32),
            pltpu.VMEM((PLANE, HS, 2 * HS), F32),
            pltpu.VMEM((4, HS, 2 * HS), F32),
            pltpu.VMEM((4,) + square, F32),
            pltpu.VMEM((PLANE,) + square, F32),
            pltpu.VMEM((2,) + square, F32),
            pltpu.VMEM((pairs,) + square, F32),
            tokens,
            pltpu.VMEM((seqs, parts, 2, SLOTS, share, cols), F32),
            line,
            line,
            line,
            pltpu.VMEM((seqs, rows // SLOTS, width), F32),
            pltpu.VMEM((seqs, rows // SLOTS, width), F32),
            pltpu.VMEM((seqs, parts, 2, share, cols), F32),
            pltpu.VMEM((seqs, parts, share, cols), F32),
            dma((10,)),
            dma((pairs,)),
            dma((PLANE,)),
            dma((PLANE,)),
            dma((pairs,)),
            dma,
            dma,
            dma((seqs, parts)),
            dma((seqs, parts)),
            dma((seqs, parts, SLOTS)),
            dma((seqs, parts, SLOTS)),
            dma((seqs, parts, SLOTS)),
            dma((seqs, parts, SLOTS)),
            dma((seqs,)),
            dma((seqs,)),
            dma((seqs, parts)),
            dma((seqs, parts)),
        ],
        compiler_params=pltpu.CompilerParams(
            collective_id=0, has_side_effects=True, vmem_limit_bytes=56 * 2**20
        ),
        name="layer",
    )(
        queries,
        keys,
        values,
        token_gate,
        head_rate.reshape(1, heads),
        init_state,
        norm_gain.reshape(1, width),
        out_proj,
    )
    straight = plan[0] == 0
    return jnp.stack(
        [jnp.where(straight, summed[0], summed[1]), jnp.where(straight, summed[1], summed[0])], axis=1
    )


def solution(mesh):
    return jax.shard_map(
        per_device,
        mesh=mesh,
        in_specs=(
            P(None, "ctx", "head"),
            P(None, "ctx", "head"),
            P(None, "ctx", "head"),
            P(None, "head", "ctx"),
            P("head"),
            P("head", None, None),
            P("head"),
            P("head", None),
            P(),
        ),
        out_specs=P(("ctx", "head"), None, None),
        check_vma=False,
    )
```

```python
import jax
import jax.numpy as jnp
from jax import lax
from jax.experimental import pallas as pl
from jax.experimental.pallas import tpu as pltpu
from jax.sharding import PartitionSpec as P

HS = 128
MB = 64
EPS = 1e-06
MESH = pl.DeviceIdType.MESH
F32 = jnp.float32
BF16 = jnp.bfloat16
PLANE = 16
SIDE = 4
HALF = 8
SLOTS = 4


def halves(a):
    hi = a.astype(BF16)
    return hi, (a - hi.astype(F32)).astype(BF16)


def mm(a, b):
    return jnp.dot(a, b, preferred_element_type=F32)


def mm3(a, b):
    return mm(a[0], b[0]) + (mm(a[0], b[1]) + mm(a[1], b[0]))


def nt(a, b):
    return lax.dot_general(a, b, (((1,), (1,)), ((), ())), preferred_element_type=F32)


def tn(a, b):
    return lax.dot_general(a, b, (((0,), (0,)), ((), ())), preferred_element_type=F32)


def spread(k, v, ecol):
    rows = k.shape[0]
    gram = nt(k, k)
    kv = jnp.concatenate([k, v], axis=1).astype(F32)
    first = halves(kv[:MB] * ecol[:MB])
    his, los = [first[0]], [first[1]]
    for start in range(MB, rows, MB):
        left = halves(gram[start : start + MB, :start])
        hi, lo = jnp.concatenate(his, axis=0), jnp.concatenate(los, axis=0)
        part = kv[start : start + MB] - mm3(left, (hi, lo))
        nxt = halves(part * ecol[start : start + MB])
        his.append(nxt[0])
        los.append(nxt[1])
    return jnp.concatenate(his, axis=0), jnp.concatenate(los, axis=0)


def slice_map(k, hi, lo):
    moved = tn(k, hi) + tn(k, lo)
    r = lax.broadcasted_iota(jnp.int32, (HS, HS), 0)
    c = lax.broadcasted_iota(jnp.int32, (HS, HS), 1)
    eye = jnp.where(r == c, 1.0, 0.0).astype(F32)
    return jnp.concatenate([eye - moved[:, :HS], moved[:, HS:]], axis=1)


def readout(q, k, hi, lo):
    rows = q.shape[0]
    scores = nt(q, k)
    r = lax.broadcasted_iota(jnp.int32, (rows, rows), 0)
    c = lax.broadcasted_iota(jnp.int32, (rows, rows), 1)
    scores = halves(jnp.where(c <= r, scores, 0.0))
    read = mm3(scores, (hi, lo))
    return q.astype(F32) - read[:, :HS], read[:, HS:]


def after(earlier, later):
    moved = mm3(halves(later[:, :HS]), halves(earlier))
    return moved + jnp.concatenate([jnp.zeros((HS, HS), F32), later[:, HS:]], axis=1)


def applied(change, state):
    return mm3(halves(change[:, :HS]), halves(state)) + change[:, HS:]


def copy_wait(ref, sem):
    pltpu.make_async_copy(ref, ref, sem).wait()


def layer_kernel(
    q_hbm, k_hbm, v_hbm, gate_hbm, rate_hbm, init_hbm, gain_hbm, proj_hbm, out_ref,
    q_ref, k_ref, v_ref, gate_ref, rate_ref, init_ref, gain_ref, proj_ref,
    ehi, elo, fd_ref, qh_ref, ql_ref, z0_ref,
    recv, total, enter, wout, chain, wbuf, normed, prod, sib, rbuf, lbuf, nout, nin, eprod, esib,
    in_sem, fd_send, fd_recv, w_send, w_recv, c_send, c_recv, t_send, t_recv,
    sib_send, sib_recv, r_send, r_recv, l_send, l_recv, n_send, n_recv, e_send, e_recv,
):
    me_c, me_h = lax.axis_index("ctx"), lax.axis_index("head")
    zhi, p = me_c // PLANE, lax.rem(me_c, PLANE)
    x, y = p // SIDE, lax.rem(p, SIDE)
    near, spot = x // 2, lax.rem(p, HALF)
    base = zhi * PLANE + near * HALF
    stage = 2 * zhi + near
    across = zhi * PLANE + lax.rem(p + HALF, PLANE)
    far_across = (1 - zhi) * PLANE + lax.rem(p + HALF, PLANE)
    z, core = me_h // 2, lax.rem(me_h, 2)
    twin = z * 2 + (1 - core)
    partner = (1 - zhi) * PLANE + p
    low, high = z == 0, z == SLOTS - 1
    end = jnp.logical_or(low, high)
    far = SLOTS - 1 - z
    left = (jnp.where(low, partner, me_c), jnp.where(low, 2 * (SLOTS - 1) + core, me_h - 2))
    right = (jnp.where(high, partner, me_c), jnp.where(high, core, me_h + 2))
    seqs, rows = q_ref.shape[0], q_ref.shape[1]
    heads = init_ref.shape[0]
    pairs = seqs * heads
    parts, width = prod.shape[1], prod.shape[-1]

    loads = []
    order = [(k_hbm.at[0], k_ref.at[0]), (v_hbm.at[0], v_ref.at[0]), (gate_hbm, gate_ref), (rate_hbm, rate_ref)]
    order += [(k_hbm.at[1], k_ref.at[1]), (v_hbm.at[1], v_ref.at[1]), (q_hbm, q_ref), (init_hbm, init_ref)]
    order += [(gain_hbm, gain_ref), (proj_hbm, proj_ref)]
    for i, (src, dst) in enumerate(order):
        loads.append(pltpu.make_async_copy(src, dst, in_sem.at[i]))
        loads[-1].start()

    barrier = pltpu.get_barrier_semaphore()
    for step in range(1, HALF):
        other = base + lax.rem(spot + step, HALF)
        pl.semaphore_signal(barrier, inc=1, device_id=(other, me_h), device_id_type=MESH)
    for other in ((partner, me_h), (across, me_h), (far_across, me_h), (me_c, twin), left, right):
        pl.semaphore_signal(barrier, inc=1, device_id=other, device_id_type=MESH)

    for i in range(4):
        loads[i].wait()
    etas = []
    for s in range(seqs):
        eta = [gate_ref[s, h : h + 1] * rate_ref[0:1, h : h + 1] for h in range(heads)]
        etas.append(jnp.concatenate(eta + [jnp.zeros((8 - heads, rows), F32)], axis=0).T)

    def home(s, h):
        return (core if s == 0 else 1 - core) * SIDE + h

    def fd_copy(s, h):
        return pltpu.make_async_remote_copy(
            src_ref=fd_ref.at[s * heads + h],
            dst_ref=recv.at[spot],
            send_sem=fd_send.at[s * heads + h],
            recv_sem=fd_recv.at[spot],
            device_id=(base + home(s, h), me_h),
            device_id_type=MESH,
        )

    def make_maps(s):
        for h in range(heads):
            cols = slice(h * HS, (h + 1) * HS)
            k = k_ref[s, :, cols]
            hi, lo = spread(k, v_ref[s, :, cols], etas[s][:, h : h + 1])
            ehi[s * heads + h] = hi
            elo[s * heads + h] = lo
            fd_ref[s * heads + h] = slice_map(k, hi, lo)

    def send_maps(s):
        for i in range(heads):
            h = lax.rem(y + i, heads)
            to = home(s, h)

            @pl.when(to != spot)
            def _():
                fd_copy(s, h).start()

            @pl.when(to == spot)
            def _():
                pltpu.make_async_copy(fd_ref.at[s * heads + h], recv.at[spot], fd_recv.at[spot]).start()

    def readouts(s):
        for h in range(heads):
            j = s * heads + h
            cols = slice(h * HS, (h + 1) * HS)
            qt, z0 = readout(q_ref[s, :, cols], k_ref[s, :, cols], ehi[j], elo[j])
            hi, lo = halves(qt)
            qh_ref[j] = hi
            ql_ref[j] = lo
            z0_ref[j] = z0

    make_maps(0)
    pl.semaphore_wait(barrier, HALF - 1 + 6)
    send_maps(0)
    loads[6].wait()
    readouts(0)
    loads[4].wait()
    loads[5].wait()
    make_maps(1)
    readouts(1)
    for load in loads[7:]:
        load.wait()

    first = lax.rem(x, 2) == core
    mine = jnp.where(first, 0, heads) + y

    def w_copy(c):
        return pltpu.make_async_remote_copy(
            src_ref=wout.at[c],
            dst_ref=wbuf.at[mine],
            send_sem=w_send.at[c],
            recv_sem=w_recv.at[mine],
            device_id=(base + c, me_h),
            device_id_type=MESH,
        )

    def chain_copy(i, to):
        return pltpu.make_async_remote_copy(
            src_ref=chain.at[0],
            dst_ref=chain.at[1],
            send_sem=c_send.at[i],
            recv_sem=c_recv,
            device_id=(to, me_h),
            device_id_type=MESH,
        )

    t_copy = pltpu.make_async_remote_copy(
        src_ref=total.at[0],
        dst_ref=total.at[1],
        send_sem=t_send,
        recv_sem=t_recv,
        device_id=(across, me_h),
        device_id_type=MESH,
    )

    def scan(s):
        @pl.when(first if s == 0 else jnp.logical_not(first))
        def _():
            for i in range(SIDE):
                for g in range(2):
                    c = SIDE * g + i
                    copy_wait(recv.at[c], fd_recv.at[c])
                    if i > 0:
                        recv[c] = after(recv[c - 1], recv[c])
            total[0] = after(recv[SIDE - 1], recv[HALF - 1])

            @pl.when(stage == 2)
            def _():
                t_copy.start()

            @pl.when(stage == 0)
            def _():
                enter[0] = init_ref[y]
                chain[0] = applied(total[0], init_ref[y])
                chain_copy(0, across).start()

            @pl.when(stage > 0)
            def _():
                copy_wait(chain.at[1], c_recv)
                enter[0] = chain[1]

            @pl.when(stage == 1)
            def _():
                chain[0] = applied(total[0], enter[0])
                chain_copy(0, far_across).start()
                chain_copy(1, partner).start()

            @pl.when(stage == 3)
            def _():
                t_copy.wait_recv()
                enter[0] = applied(total[1], chain[1])

            enter[1] = applied(recv[SIDE - 1], enter[0])
            for i in range(2):
                g = lax.rem(x + i, 2)
                wout[SIDE * g] = enter[g]
                for k in range(1, SIDE):
                    wout[SIDE * g + k] = applied(recv[SIDE * g + k - 1], enter[g])
                for i2 in range(SIDE):
                    c = SIDE * g + lax.rem(y + i2, SIDE)

                    @pl.when(c != spot)
                    def _():
                        w_copy(c).start()

                    @pl.when(c == spot)
                    def _():
                        pltpu.make_async_copy(wout.at[c], wbuf.at[mine], w_recv.at[mine]).start()

    def sib_copy(s, q):
        return pltpu.make_async_remote_copy(
            src_ref=prod.at[s, q, 1 - core],
            dst_ref=sib.at[s, q],
            send_sem=sib_send.at[s, q],
            recv_sem=sib_recv.at[s, q],
            device_id=(me_c, twin),
            device_id_type=MESH,
        )

    def line_copy(s, q, b, src, toward_right):
        buf, send, got = (rbuf, r_send, r_recv) if toward_right else (lbuf, l_send, l_recv)
        return pltpu.make_async_remote_copy(
            src_ref=src,
            dst_ref=buf.at[s, q, b],
            send_sem=send.at[s, q, b],
            recv_sem=got.at[s, q, b],
            device_id=right if toward_right else left,
            device_id_type=MESH,
        )

    def own_copy(s, q, b, toward_right):
        return line_copy(s, q, b, prod.at[s, q, core, b], toward_right)

    def far_copy(s, q, toward_right):
        return line_copy(s, q, far, eprod.at[s, q, core], toward_right)

    def rows_copy(s):
        return pltpu.make_async_remote_copy(
            src_ref=nout.at[s],
            dst_ref=nin.at[s],
            send_sem=n_send.at[s],
            recv_sem=n_recv.at[s],
            device_id=(partner, me_h),
            device_id_type=MESH,
        )

    def twin_copy(s, q):
        return pltpu.make_async_remote_copy(
            src_ref=eprod.at[s, q, 1 - core],
            dst_ref=esib.at[s, q],
            send_sem=e_send.at[s, q],
            recv_sem=e_recv.at[s, q],
            device_id=(me_c, twin),
            device_id_type=MESH,
        )

    def each(body):
        lax.fori_loop(0, parts, lambda q, carry: (body(q), carry)[1], 0)

    block = rows // SLOTS
    half = block // 2

    def outputs(s):
        for j in range(s * heads, (s + 1) * heads):
            copy_wait(wbuf.at[j], w_recv.at[j])
        if s == 0:
            send_maps(1)
        for h in range(heads):
            j = s * heads + h
            cols = slice(h * HS, (h + 1) * HS)
            zval = mm3((qh_ref[j], ql_ref[j]), halves(wbuf[j])) + z0_ref[j]
            scale = lax.rsqrt(jnp.mean(zval * zval, axis=-1, keepdims=True) + EPS)
            normed[s, :, cols] = (zval * scale * gain_ref[:, cols]).astype(BF16)

        @pl.when(end)
        def _():
            start = pl.multiple_of(far * block, block)
            nout[s] = normed[s, pl.ds(start, block), :].astype(F32)
            rows_copy(s).start()

        def project(q):
            start = pl.multiple_of(q * width, width)
            part = mm(normed[s], proj_ref[:, pl.ds(start, width)])
            part = part.reshape(SLOTS, 2, half, width)
            prod[s, q, 0] = part[:, 0]
            prod[s, q, 1] = part[:, 1]
            sib_copy(s, q).start()

        def pair_sum(q):
            sib_copy(s, q).wait_recv()
            sib_copy(s, q).wait_send()
            for b in range(SLOTS):
                prod[s, q, core, b] += sib[s, q, b]

            @pl.when(z == 0)
            def _():
                own_copy(s, q, 2, True).start()

            @pl.when(z == 1)
            def _():
                own_copy(s, q, 3, True).start()

            @pl.when(z == 2)
            def _():
                own_copy(s, q, 0, False).start()

            @pl.when(z == 3)
            def _():
                own_copy(s, q, 1, False).start()

        def both(q):
            project(q)
            pair_sum(q - 1)

        project(0)
        lax.fori_loop(1, parts, lambda q, carry: (both(q), carry)[1], 0)
        pair_sum(parts - 1)

    def nearest(s):
        def rightward(q):
            own_copy(s, q, 2, True).wait_send()
            own_copy(s, q, 1, True).start()

        def leftward(q):
            own_copy(s, q, 1, False).wait_send()
            own_copy(s, q, 2, False).start()

        @pl.when(z == 0)
        def _():
            each(rightward)

        @pl.when(z == 3)
        def _():
            each(leftward)

    def far_rows(s):
        @pl.when(end)
        def _():
            copy_wait(nin.at[s], n_recv.at[s])
            there = nin[s].astype(BF16)

            def project(q):
                start = pl.multiple_of(q * width, width)
                part = mm(there, proj_ref[:, pl.ds(start, width)])
                eprod[s, q] = part.reshape(2, half, width)
                twin_copy(s, q).start()

            each(project)

            def pair_sum(q):
                twin_copy(s, q).wait_recv()
                eprod[s, q, core] += esib[s, q]

                @pl.when(low)
                def _():
                    far_copy(s, q, False).start()

                @pl.when(high)
                def _():
                    far_copy(s, q, True).start()

            each(pair_sum)

    def take(s, q, b, buf, got):
        copy_wait(buf.at[s, q, b], got.at[s, q, b])
        prod[s, q, core, b] += buf[s, q, b]

    def forwards(s):
        def up(q):
            take(s, q, 2, rbuf, r_recv)
            own_copy(s, q, 2, True).start()
            take(s, q, 0, lbuf, l_recv)
            own_copy(s, q, 0, False).start()

        def down(q):
            take(s, q, 1, lbuf, l_recv)
            own_copy(s, q, 1, False).start()
            take(s, q, 3, rbuf, r_recv)
            own_copy(s, q, 3, True).start()

        @pl.when(z == 1)
        def _():
            each(up)

        @pl.when(z == 2)
        def _():
            each(down)

    def finals(s):
        for q in range(parts):
            take(s, q, z, rbuf, r_recv)
            take(s, q, z, lbuf, l_recv)
            out_ref[s, :, q * width : (q + 1) * width] = prod[s, q, core, z].astype(BF16)

    scan(0)
    outputs(0)
    far_rows(0)
    scan(1)
    nearest(0)
    forwards(0)
    outputs(1)
    far_rows(1)
    nearest(1)
    finals(0)
    forwards(1)
    finals(1)

    def finish(i, carry):
        s, q = i // parts, lax.rem(i, parts)

        @pl.when(z == 0)
        def _():
            own_copy(s, q, 1, True).wait_send()
            far_copy(s, q, False).wait_send()

        @pl.when(z == 1)
        def _():
            own_copy(s, q, 3, True).wait_send()
            own_copy(s, q, 2, True).wait_send()
            own_copy(s, q, 0, False).wait_send()

        @pl.when(z == 2)
        def _():
            own_copy(s, q, 0, False).wait_send()
            own_copy(s, q, 1, False).wait_send()
            own_copy(s, q, 3, True).wait_send()

        @pl.when(z == 3)
        def _():
            own_copy(s, q, 2, False).wait_send()
            far_copy(s, q, True).wait_send()

        @pl.when(end)
        def _():
            twin_copy(s, q).wait_send()

        return carry

    lax.fori_loop(0, seqs * parts, finish, 0)

    @pl.when(end)
    def _():
        for s in range(seqs):
            rows_copy(s).wait_send()

    for j in range(pairs):

        @pl.when(home(j // heads, j % heads) != spot)
        def _():
            fd_copy(j // heads, j % heads).wait_send()

    def done(c, carry):
        @pl.when(c != spot)
        def _():
            w_copy(c).wait_send()

        return carry

    lax.fori_loop(0, HALF, done, 0)

    @pl.when(stage == 0)
    def _():
        chain_copy(0, across).wait_send()

    @pl.when(stage == 1)
    def _():
        chain_copy(0, far_across).wait_send()
        chain_copy(1, partner).wait_send()

    @pl.when(stage == 2)
    def _():
        t_copy.wait_send()


def per_device(queries, keys, values, token_gate, head_rate, init_state, norm_gain, out_proj, plan):
    seqs, rows, width = queries.shape
    heads = init_state.shape[0]
    pairs = seqs * heads
    model = out_proj.shape[1]
    parts = 4
    cols = model // parts
    share = rows // (2 * SLOTS)
    dma = pltpu.SemaphoreType.DMA
    tokens = pltpu.VMEM((seqs, rows, width), BF16)
    line = pltpu.VMEM((seqs, parts, SLOTS, share, cols), F32)
    square = (HS, HS)
    summed = pl.pallas_call(
        layer_kernel,
        out_shape=jax.ShapeDtypeStruct((seqs, share, model), BF16),
        in_specs=[pl.BlockSpec(memory_space=pltpu.HBM)] * 8,
        out_specs=pl.BlockSpec(memory_space=pltpu.VMEM),
        scratch_shapes=[
            tokens,
            tokens,
            tokens,
            pltpu.VMEM((seqs, heads, rows), F32),
            pltpu.VMEM((1, heads), F32),
            pltpu.VMEM((heads,) + square, F32),
            pltpu.VMEM((1, width), F32),
            pltpu.VMEM((width, model), BF16),
            pltpu.VMEM((pairs, rows, 2 * HS), BF16),
            pltpu.VMEM((pairs, rows, 2 * HS), BF16),
            pltpu.VMEM((pairs, HS, 2 * HS), F32),
            pltpu.VMEM((pairs, rows, HS), BF16),
            pltpu.VMEM((pairs, rows, HS), BF16),
            pltpu.VMEM((pairs, rows, HS), F32),
            pltpu.VMEM((HALF, HS, 2 * HS), F32),
            pltpu.VMEM((2, HS, 2 * HS), F32),
            pltpu.VMEM((2,) + square, F32),
            pltpu.VMEM((HALF,) + square, F32),
            pltpu.VMEM((2,) + square, F32),
            pltpu.VMEM((pairs,) + square, F32),
            tokens,
            pltpu.VMEM((seqs, parts, 2, SLOTS, share, cols), F32),
            line,
            line,
            line,
            pltpu.VMEM((seqs, rows // SLOTS, width), F32),
            pltpu.VMEM((seqs, rows // SLOTS, width), F32),
            pltpu.VMEM((seqs, parts, 2, share, cols), F32),
            pltpu.VMEM((seqs, parts, share, cols), F32),
            dma((10,)),
            dma((pairs,)),
            dma((HALF,)),
            dma((HALF,)),
            dma((pairs,)),
            dma((2,)),
            dma,
            dma,
            dma,
            dma((seqs, parts)),
            dma((seqs, parts)),
            dma((seqs, parts, SLOTS)),
            dma((seqs, parts, SLOTS)),
            dma((seqs, parts, SLOTS)),
            dma((seqs, parts, SLOTS)),
            dma((seqs,)),
            dma((seqs,)),
            dma((seqs, parts)),
            dma((seqs, parts)),
        ],
        compiler_params=pltpu.CompilerParams(
            collective_id=0, has_side_effects=True, vmem_limit_bytes=56 * 2**20
        ),
        name="layer",
    )(
        queries,
        keys,
        values,
        token_gate,
        head_rate.reshape(1, heads),
        init_state,
        norm_gain.reshape(1, width),
        out_proj,
    )
    straight = plan[0] == 0
    return jnp.stack(
        [jnp.where(straight, summed[0], summed[1]), jnp.where(straight, summed[1], summed[0])], axis=1
    )


def solution(mesh):
    return jax.shard_map(
        per_device,
        mesh=mesh,
        in_specs=(
            P(None, "ctx", "head"),
            P(None, "ctx", "head"),
            P(None, "ctx", "head"),
            P(None, "head", "ctx"),
            P("head"),
            P("head", None, None),
            P("head"),
            P("head", None),
            P(),
        ),
        out_specs=P(("ctx", "head"), None, None),
        check_vma=False,
    )
```

```python
import jax
import jax.numpy as jnp
from jax import lax
from jax.experimental import pallas as pl
from jax.experimental.pallas import tpu as pltpu
from jax.sharding import PartitionSpec as P

HS = 128
MB = 64
EPS = 1e-06
MESH = pl.DeviceIdType.MESH
F32 = jnp.float32
BF16 = jnp.bfloat16
PLANE = 16
SIDE = 4
HALF = 8
SLOTS = 4


def halves(a):
    hi = a.astype(BF16)
    return hi, (a - hi.astype(F32)).astype(BF16)


def mm(a, b):
    return jnp.dot(a, b, preferred_element_type=F32)


def mm3(a, b):
    return mm(a[0], b[0]) + (mm(a[0], b[1]) + mm(a[1], b[0]))


def nt(a, b):
    return lax.dot_general(a, b, (((1,), (1,)), ((), ())), preferred_element_type=F32)


def tn(a, b):
    return lax.dot_general(a, b, (((0,), (0,)), ((), ())), preferred_element_type=F32)


def spread(k, v, ecol):
    rows = k.shape[0]
    gram = nt(k, k)
    kv = jnp.concatenate([k, v], axis=1).astype(F32)
    first = halves(kv[:MB] * ecol[:MB])
    his, los = [first[0]], [first[1]]
    for start in range(MB, rows, MB):
        left = halves(gram[start : start + MB, :start])
        hi, lo = jnp.concatenate(his, axis=0), jnp.concatenate(los, axis=0)
        part = kv[start : start + MB] - mm3(left, (hi, lo))
        nxt = halves(part * ecol[start : start + MB])
        his.append(nxt[0])
        los.append(nxt[1])
    return jnp.concatenate(his, axis=0), jnp.concatenate(los, axis=0)


def slice_map(k, hi, lo):
    moved = tn(k, hi) + tn(k, lo)
    r = lax.broadcasted_iota(jnp.int32, (HS, HS), 0)
    c = lax.broadcasted_iota(jnp.int32, (HS, HS), 1)
    eye = jnp.where(r == c, 1.0, 0.0).astype(F32)
    return jnp.concatenate([eye - moved[:, :HS], moved[:, HS:]], axis=1)


def readout(q, k, hi, lo):
    rows = q.shape[0]
    scores = nt(q, k)
    r = lax.broadcasted_iota(jnp.int32, (rows, rows), 0)
    c = lax.broadcasted_iota(jnp.int32, (rows, rows), 1)
    scores = halves(jnp.where(c <= r, scores, 0.0))
    read = mm3(scores, (hi, lo))
    return q.astype(F32) - read[:, :HS], read[:, HS:]


def after(earlier, later):
    moved = mm3(halves(later[:, :HS]), halves(earlier))
    return moved + jnp.concatenate([jnp.zeros((HS, HS), F32), later[:, HS:]], axis=1)


def applied(change, state):
    return mm3(halves(change[:, :HS]), halves(state)) + change[:, HS:]


def copy_wait(ref, sem):
    pltpu.make_async_copy(ref, ref, sem).wait()


def layer_kernel(
    q_hbm, k_hbm, v_hbm, gate_hbm, rate_hbm, init_hbm, gain_hbm, plan_hbm, proj_hbm, out_ref,
    q_ref, k_ref, v_ref, gate_ref, rate_ref, init_ref, gain_ref, plan_ref, proj_ref,
    ehi, elo, fd_ref, qh_ref, ql_ref, z0_ref,
    done_first, recv, total, enter, wout, chain, wbuf, normed, prod, sib, rbuf, lbuf, nout, nin, eprod, esib,
    in_sem, fd_send, fd_recv, w_send, w_recv, c_send, c_recv, t_send, t_recv, m_send, m_recv,
    sib_send, sib_recv, r_send, r_recv, l_send, l_recv, n_send, n_recv, e_send, e_recv,
):
    me_c, me_h = lax.axis_index("ctx"), lax.axis_index("head")
    zhi, p = me_c // PLANE, lax.rem(me_c, PLANE)
    x, y = p // SIDE, lax.rem(p, SIDE)
    near, spot = x // 2, lax.rem(p, HALF)
    base = zhi * PLANE + near * HALF
    stage = 2 * zhi + near
    across = zhi * PLANE + lax.rem(p + HALF, PLANE)
    far_across = (1 - zhi) * PLANE + lax.rem(p + HALF, PLANE)
    z, core = me_h // 2, lax.rem(me_h, 2)
    twin = z * 2 + (1 - core)
    partner = (1 - zhi) * PLANE + p
    low, high = z == 0, z == SLOTS - 1
    end = jnp.logical_or(low, high)
    far = SLOTS - 1 - z
    left = (jnp.where(low, partner, me_c), jnp.where(low, 2 * (SLOTS - 1) + core, me_h - 2))
    right = (jnp.where(high, partner, me_c), jnp.where(high, core, me_h + 2))
    seqs, rows = q_ref.shape[0], q_ref.shape[1]
    heads = init_ref.shape[0]
    pairs = seqs * heads
    parts, width = prod.shape[1], prod.shape[-1]

    loads = []
    order = [(k_hbm.at[0], k_ref.at[0]), (v_hbm.at[0], v_ref.at[0]), (gate_hbm, gate_ref), (rate_hbm, rate_ref)]
    order += [(k_hbm.at[1], k_ref.at[1]), (v_hbm.at[1], v_ref.at[1]), (q_hbm, q_ref), (init_hbm, init_ref)]
    order += [(gain_hbm, gain_ref), (plan_hbm, plan_ref), (proj_hbm, proj_ref)]
    for i, (src, dst) in enumerate(order):
        loads.append(pltpu.make_async_copy(src, dst, in_sem.at[i]))
        loads[-1].start()

    barrier = pltpu.get_barrier_semaphore()
    for step in range(1, HALF):
        other = base + lax.rem(spot + step, HALF)
        pl.semaphore_signal(barrier, inc=1, device_id=(other, me_h), device_id_type=MESH)
    for other in ((partner, me_h), (across, me_h), (far_across, me_h), (me_c, twin), left, right):
        pl.semaphore_signal(barrier, inc=1, device_id=other, device_id_type=MESH)

    for i in range(4):
        loads[i].wait()
    etas = []
    for s in range(seqs):
        eta = [gate_ref[s, h : h + 1] * rate_ref[0:1, h : h + 1] for h in range(heads)]
        etas.append(jnp.concatenate(eta + [jnp.zeros((8 - heads, rows), F32)], axis=0).T)

    def home(s, h):
        return (core if s == 0 else 1 - core) * SIDE + h

    def fd_copy(s, h):
        return pltpu.make_async_remote_copy(
            src_ref=fd_ref.at[s * heads + h],
            dst_ref=recv.at[spot],
            send_sem=fd_send.at[s * heads + h],
            recv_sem=fd_recv.at[spot],
            device_id=(base + home(s, h), me_h),
            device_id_type=MESH,
        )

    def make_maps(s):
        for h in range(heads):
            cols = slice(h * HS, (h + 1) * HS)
            k = k_ref[s, :, cols]
            hi, lo = spread(k, v_ref[s, :, cols], etas[s][:, h : h + 1])
            ehi[s * heads + h] = hi
            elo[s * heads + h] = lo
            fd_ref[s * heads + h] = slice_map(k, hi, lo)

    def send_maps(s):
        for i in range(heads):
            h = lax.rem(y + i, heads)
            to = home(s, h)

            @pl.when(to != spot)
            def _():
                fd_copy(s, h).start()

            @pl.when(to == spot)
            def _():
                pltpu.make_async_copy(fd_ref.at[s * heads + h], recv.at[spot], fd_recv.at[spot]).start()

    def readouts(s):
        for h in range(heads):
            j = s * heads + h
            cols = slice(h * HS, (h + 1) * HS)
            qt, z0 = readout(q_ref[s, :, cols], k_ref[s, :, cols], ehi[j], elo[j])
            hi, lo = halves(qt)
            qh_ref[j] = hi
            ql_ref[j] = lo
            z0_ref[j] = z0

    make_maps(0)
    pl.semaphore_wait(barrier, HALF - 1 + 6)
    send_maps(0)
    loads[6].wait()
    readouts(0)
    loads[4].wait()
    loads[5].wait()
    make_maps(1)
    readouts(1)
    for load in loads[7:]:
        load.wait()

    first = lax.rem(x, 2) == core
    mine = jnp.where(first, 0, heads) + y

    def w_copy(c):
        return pltpu.make_async_remote_copy(
            src_ref=wout.at[c],
            dst_ref=wbuf.at[mine],
            send_sem=w_send.at[c],
            recv_sem=w_recv.at[mine],
            device_id=(base + c, me_h),
            device_id_type=MESH,
        )

    def chain_copy(i, to):
        return pltpu.make_async_remote_copy(
            src_ref=chain.at[0],
            dst_ref=chain.at[1],
            send_sem=c_send.at[i],
            recv_sem=c_recv,
            device_id=(to, me_h),
            device_id_type=MESH,
        )

    def map_copy(i, to):
        return pltpu.make_async_remote_copy(
            src_ref=total.at[0],
            dst_ref=total.at[2],
            send_sem=m_send.at[i],
            recv_sem=m_recv,
            device_id=(to, me_h),
            device_id_type=MESH,
        )

    t_copy = pltpu.make_async_remote_copy(
        src_ref=total.at[0],
        dst_ref=total.at[1],
        send_sem=t_send,
        recv_sem=t_recv,
        device_id=(across, me_h),
        device_id_type=MESH,
    )

    def scan(s):
        @pl.when(first if s == 0 else jnp.logical_not(first))
        def _():
            for i in range(SIDE):
                for g in range(2):
                    c = SIDE * g + i
                    copy_wait(recv.at[c], fd_recv.at[c])
                    if i > 0:
                        recv[c] = after(recv[c - 1], recv[c])
            total[0] = after(recv[SIDE - 1], recv[HALF - 1])

            @pl.when(stage == 2)
            def _():
                t_copy.start()

            @pl.when(stage == 0)
            def _():
                enter[0] = init_ref[y]
                chain[0] = applied(total[0], init_ref[y])
                if s == 0:
                    chain_copy(1, far_across).start()
                    chain_copy(2, partner).start()
                chain_copy(0, across).start()

            if s == 0:

                @pl.when(stage == 1)
                def _():
                    map_copy(0, far_across).start()
                    map_copy(1, partner).start()

            @pl.when(stage > 0)
            def _():
                copy_wait(chain.at[1], c_recv)
                enter[0] = chain[1]

            if s == 0:

                @pl.when(stage > 1)
                def _():
                    copy_wait(total.at[2], m_recv)
                    enter[0] = applied(total[2], chain[1])

            else:

                @pl.when(stage == 1)
                def _():
                    chain[0] = applied(total[0], enter[0])
                    chain_copy(0, far_across).start()
                    chain_copy(1, partner).start()

            @pl.when(stage == 3)
            def _():
                t_copy.wait_recv()
                enter[0] = applied(total[1], enter[0])

            enter[1] = applied(recv[SIDE - 1], enter[0])
            for i in range(2):
                g = lax.rem(x + i, 2)
                wout[SIDE * g] = enter[g]
                for k in range(1, SIDE):
                    wout[SIDE * g + k] = applied(recv[SIDE * g + k - 1], enter[g])
                for i2 in range(SIDE):
                    c = SIDE * g + lax.rem(y + i2, SIDE)

                    @pl.when(c != spot)
                    def _():
                        w_copy(c).start()

                    @pl.when(c == spot)
                    def _():
                        pltpu.make_async_copy(wout.at[c], wbuf.at[mine], w_recv.at[mine]).start()

    def sib_copy(s, q):
        return pltpu.make_async_remote_copy(
            src_ref=prod.at[s, q, 1 - core],
            dst_ref=sib.at[s, q],
            send_sem=sib_send.at[s, q],
            recv_sem=sib_recv.at[s, q],
            device_id=(me_c, twin),
            device_id_type=MESH,
        )

    def line_copy(s, q, b, src, toward_right):
        buf, send, got = (rbuf, r_send, r_recv) if toward_right else (lbuf, l_send, l_recv)
        return pltpu.make_async_remote_copy(
            src_ref=src,
            dst_ref=buf.at[s, q, b],
            send_sem=send.at[s, q, b],
            recv_sem=got.at[s, q, b],
            device_id=right if toward_right else left,
            device_id_type=MESH,
        )

    def own_copy(s, q, b, toward_right):
        return line_copy(s, q, b, prod.at[s, q, core, b], toward_right)

    def far_copy(s, q, toward_right):
        return line_copy(s, q, far, eprod.at[s, q, core], toward_right)

    def rows_copy(s):
        return pltpu.make_async_remote_copy(
            src_ref=nout.at[s],
            dst_ref=nin.at[s],
            send_sem=n_send.at[s],
            recv_sem=n_recv.at[s],
            device_id=(partner, me_h),
            device_id_type=MESH,
        )

    def twin_copy(s, q):
        return pltpu.make_async_remote_copy(
            src_ref=eprod.at[s, q, 1 - core],
            dst_ref=esib.at[s, q],
            send_sem=e_send.at[s, q],
            recv_sem=e_recv.at[s, q],
            device_id=(me_c, twin),
            device_id_type=MESH,
        )

    def each(body):
        lax.fori_loop(0, parts, lambda q, carry: (body(q), carry)[1], 0)

    block = rows // SLOTS
    half = block // 2

    def outputs(s):
        for j in range(s * heads, (s + 1) * heads):
            copy_wait(wbuf.at[j], w_recv.at[j])
        if s == 0:
            send_maps(1)
        for h in range(heads):
            j = s * heads + h
            cols = slice(h * HS, (h + 1) * HS)
            zval = mm3((qh_ref[j], ql_ref[j]), halves(wbuf[j])) + z0_ref[j]
            scale = lax.rsqrt(jnp.mean(zval * zval, axis=-1, keepdims=True) + EPS)
            normed[s, :, cols] = (zval * scale * gain_ref[:, cols]).astype(BF16)

        @pl.when(end)
        def _():
            start = pl.multiple_of(far * block, block)
            nout[s] = normed[s, pl.ds(start, block), :].astype(F32)
            rows_copy(s).start()

        def project(q):
            start = pl.multiple_of(q * width, width)
            part = mm(normed[s], proj_ref[:, pl.ds(start, width)])
            part = part.reshape(SLOTS, 2, half, width)
            prod[s, q, 0] = part[:, 0]
            prod[s, q, 1] = part[:, 1]
            sib_copy(s, q).start()

        def pair_sum(q):
            sib_copy(s, q).wait_recv()
            sib_copy(s, q).wait_send()
            for b in range(SLOTS):
                prod[s, q, core, b] += sib[s, q, b]

            @pl.when(z == 0)
            def _():
                own_copy(s, q, 2, True).start()

            @pl.when(z == 1)
            def _():
                own_copy(s, q, 3, True).start()

            @pl.when(z == 2)
            def _():
                own_copy(s, q, 0, False).start()

            @pl.when(z == 3)
            def _():
                own_copy(s, q, 1, False).start()

        def both(q):
            project(q)
            pair_sum(q - 1)

        project(0)
        lax.fori_loop(1, parts, lambda q, carry: (both(q), carry)[1], 0)
        pair_sum(parts - 1)

    def nearest(s):
        def rightward(q):
            own_copy(s, q, 2, True).wait_send()
            own_copy(s, q, 1, True).start()

        def leftward(q):
            own_copy(s, q, 1, False).wait_send()
            own_copy(s, q, 2, False).start()

        @pl.when(z == 0)
        def _():
            each(rightward)

        @pl.when(z == 3)
        def _():
            each(leftward)

    def far_rows(s):
        @pl.when(end)
        def _():
            copy_wait(nin.at[s], n_recv.at[s])
            there = nin[s].astype(BF16)

            def project(q):
                start = pl.multiple_of(q * width, width)
                part = mm(there, proj_ref[:, pl.ds(start, width)])
                eprod[s, q] = part.reshape(2, half, width)
                twin_copy(s, q).start()

            each(project)

            def pair_sum(q):
                twin_copy(s, q).wait_recv()
                eprod[s, q, core] += esib[s, q]

                @pl.when(low)
                def _():
                    far_copy(s, q, False).start()

                @pl.when(high)
                def _():
                    far_copy(s, q, True).start()

            each(pair_sum)

    def take(s, q, b, buf, got):
        copy_wait(buf.at[s, q, b], got.at[s, q, b])
        prod[s, q, core, b] += buf[s, q, b]

    def forwards(s):
        def up(q):
            take(s, q, 2, rbuf, r_recv)
            own_copy(s, q, 2, True).start()
            take(s, q, 0, lbuf, l_recv)
            own_copy(s, q, 0, False).start()

        def down(q):
            take(s, q, 1, lbuf, l_recv)
            own_copy(s, q, 1, False).start()
            take(s, q, 3, rbuf, r_recv)
            own_copy(s, q, 3, True).start()

        @pl.when(z == 1)
        def _():
            each(up)

        @pl.when(z == 2)
        def _():
            each(down)

    def finals(s):
        for q in range(parts):
            take(s, q, z, rbuf, r_recv)
            take(s, q, z, lbuf, l_recv)
            value = prod[s, q, core, z]
            cols = slice(q * width, (q + 1) * width)
            if s == 0:
                done_first[:, cols] = value
            else:
                other = done_first[:, cols]
                straight = plan_ref[0:1, 0:1] == 0
                out_ref[:, 0, cols] = jnp.where(straight, other, value)
                out_ref[:, 1, cols] = jnp.where(straight, value, other)

    scan(0)
    outputs(0)
    far_rows(0)
    scan(1)
    nearest(0)
    forwards(0)
    outputs(1)
    far_rows(1)
    nearest(1)
    finals(0)
    forwards(1)
    finals(1)

    def finish(i, carry):
        s, q = i // parts, lax.rem(i, parts)

        @pl.when(z == 0)
        def _():
            own_copy(s, q, 1, True).wait_send()
            far_copy(s, q, False).wait_send()

        @pl.when(z == 1)
        def _():
            own_copy(s, q, 3, True).wait_send()
            own_copy(s, q, 2, True).wait_send()
            own_copy(s, q, 0, False).wait_send()

        @pl.when(z == 2)
        def _():
            own_copy(s, q, 0, False).wait_send()
            own_copy(s, q, 1, False).wait_send()
            own_copy(s, q, 3, True).wait_send()

        @pl.when(z == 3)
        def _():
            own_copy(s, q, 2, False).wait_send()
            far_copy(s, q, True).wait_send()

        @pl.when(end)
        def _():
            twin_copy(s, q).wait_send()

        return carry

    lax.fori_loop(0, seqs * parts, finish, 0)

    @pl.when(end)
    def _():
        for s in range(seqs):
            rows_copy(s).wait_send()

    for j in range(pairs):

        @pl.when(home(j // heads, j % heads) != spot)
        def _():
            fd_copy(j // heads, j % heads).wait_send()

    def done(c, carry):
        @pl.when(c != spot)
        def _():
            w_copy(c).wait_send()

        return carry

    lax.fori_loop(0, HALF, done, 0)

    @pl.when(stage == 0)
    def _():
        chain_copy(0, across).wait_send()

        @pl.when(first)
        def _():
            chain_copy(1, far_across).wait_send()
            chain_copy(2, partner).wait_send()

    @pl.when(jnp.logical_and(stage == 1, first))
    def _():
        map_copy(0, far_across).wait_send()
        map_copy(1, partner).wait_send()

    @pl.when(jnp.logical_and(stage == 1, jnp.logical_not(first)))
    def _():
        chain_copy(0, far_across).wait_send()
        chain_copy(1, partner).wait_send()

    @pl.when(stage == 2)
    def _():
        t_copy.wait_send()


def per_device(queries, keys, values, token_gate, head_rate, init_state, norm_gain, out_proj, plan):
    seqs, rows, width = queries.shape
    heads = init_state.shape[0]
    pairs = seqs * heads
    model = out_proj.shape[1]
    parts = 4
    cols = model // parts
    share = rows // (2 * SLOTS)
    dma = pltpu.SemaphoreType.DMA
    tokens = pltpu.VMEM((seqs, rows, width), BF16)
    line = pltpu.VMEM((seqs, parts, SLOTS, share, cols), F32)
    square = (HS, HS)
    summed = pl.pallas_call(
        layer_kernel,
        out_shape=jax.ShapeDtypeStruct((share, seqs, model), F32),
        in_specs=[pl.BlockSpec(memory_space=pltpu.HBM)] * 9,
        out_specs=pl.BlockSpec(memory_space=pltpu.VMEM),
        scratch_shapes=[
            tokens,
            tokens,
            tokens,
            pltpu.VMEM((seqs, heads, rows), F32),
            pltpu.VMEM((1, heads), F32),
            pltpu.VMEM((heads,) + square, F32),
            pltpu.VMEM((1, width), F32),
            pltpu.VMEM((1, seqs), jnp.int32),
            pltpu.VMEM((width, model), BF16),
            pltpu.VMEM((pairs, rows, 2 * HS), BF16),
            pltpu.VMEM((pairs, rows, 2 * HS), BF16),
            pltpu.VMEM((pairs, HS, 2 * HS), F32),
            pltpu.VMEM((pairs, rows, HS), BF16),
            pltpu.VMEM((pairs, rows, HS), BF16),
            pltpu.VMEM((pairs, rows, HS), F32),
            pltpu.VMEM((share, model), F32),
            pltpu.VMEM((HALF, HS, 2 * HS), F32),
            pltpu.VMEM((3, HS, 2 * HS), F32),
            pltpu.VMEM((2,) + square, F32),
            pltpu.VMEM((HALF,) + square, F32),
            pltpu.VMEM((2,) + square, F32),
            pltpu.VMEM((pairs,) + square, F32),
            tokens,
            pltpu.VMEM((seqs, parts, 2, SLOTS, share, cols), F32),
            line,
            line,
            line,
            pltpu.VMEM((seqs, rows // SLOTS, width), F32),
            pltpu.VMEM((seqs, rows // SLOTS, width), F32),
            pltpu.VMEM((seqs, parts, 2, share, cols), F32),
            pltpu.VMEM((seqs, parts, share, cols), F32),
            dma((11,)),
            dma((pairs,)),
            dma((HALF,)),
            dma((HALF,)),
            dma((pairs,)),
            dma((3,)),
            dma,
            dma,
            dma,
            dma((2,)),
            dma,
            dma((seqs, parts)),
            dma((seqs, parts)),
            dma((seqs, parts, SLOTS)),
            dma((seqs, parts, SLOTS)),
            dma((seqs, parts, SLOTS)),
            dma((seqs, parts, SLOTS)),
            dma((seqs,)),
            dma((seqs,)),
            dma((seqs, parts)),
            dma((seqs, parts)),
        ],
        compiler_params=pltpu.CompilerParams(
            collective_id=0, has_side_effects=True, vmem_limit_bytes=56 * 2**20
        ),
        name="layer",
    )(
        queries,
        keys,
        values,
        token_gate,
        head_rate.reshape(1, heads),
        init_state,
        norm_gain.reshape(1, width),
        plan.reshape(1, seqs),
        out_proj,
    )
    return summed.astype(BF16)


def solution(mesh):
    return jax.shard_map(
        per_device,
        mesh=mesh,
        in_specs=(
            P(None, "ctx", "head"),
            P(None, "ctx", "head"),
            P(None, "ctx", "head"),
            P(None, "head", "ctx"),
            P("head"),
            P("head", None, None),
            P("head"),
            P("head", None),
            P(),
        ),
        out_specs=P(("ctx", "head"), None, None),
        check_vma=False,
    )
```

```python
import jax
import jax.numpy as jnp
from jax import lax
from jax.experimental import pallas as pl
from jax.experimental.pallas import tpu as pltpu
from jax.sharding import PartitionSpec as P

HS = 128
MB = 64
EPS = 1e-06
MESH = pl.DeviceIdType.MESH
F32 = jnp.float32
BF16 = jnp.bfloat16
PLANE = 16
SIDE = 4
HALF = 8
SLOTS = 4


def halves(a):
    hi = a.astype(BF16)
    return hi, (a - hi.astype(F32)).astype(BF16)


def mm(a, b):
    return jnp.dot(a, b, preferred_element_type=F32)


def mm3(a, b):
    return mm(a[0], b[0]) + (mm(a[0], b[1]) + mm(a[1], b[0]))


def nt(a, b):
    return lax.dot_general(a, b, (((1,), (1,)), ((), ())), preferred_element_type=F32)


def tn(a, b):
    return lax.dot_general(a, b, (((0,), (0,)), ((), ())), preferred_element_type=F32)


def spread(k, v, ecol):
    rows = k.shape[0]
    gram = nt(k, k)
    kv = jnp.concatenate([k, v], axis=1).astype(F32)
    first = halves(kv[:MB] * ecol[:MB])
    his, los = [first[0]], [first[1]]
    for start in range(MB, rows, MB):
        left = halves(gram[start : start + MB, :start])
        hi, lo = jnp.concatenate(his, axis=0), jnp.concatenate(los, axis=0)
        part = kv[start : start + MB] - mm3(left, (hi, lo))
        nxt = halves(part * ecol[start : start + MB])
        his.append(nxt[0])
        los.append(nxt[1])
    return jnp.concatenate(his, axis=0), jnp.concatenate(los, axis=0)


def slice_map(k, hi, lo):
    moved = tn(k, hi) + tn(k, lo)
    r = lax.broadcasted_iota(jnp.int32, (HS, HS), 0)
    c = lax.broadcasted_iota(jnp.int32, (HS, HS), 1)
    eye = jnp.where(r == c, 1.0, 0.0).astype(F32)
    return jnp.concatenate([eye - moved[:, :HS], moved[:, HS:]], axis=1)


def readout(q, k, hi, lo):
    rows = q.shape[0]
    scores = nt(q, k)
    r = lax.broadcasted_iota(jnp.int32, (rows, rows), 0)
    c = lax.broadcasted_iota(jnp.int32, (rows, rows), 1)
    scores = halves(jnp.where(c <= r, scores, 0.0))
    read = mm3(scores, (hi, lo))
    return q.astype(F32) - read[:, :HS], read[:, HS:]


def after(earlier, later):
    moved = mm3(halves(later[:, :HS]), halves(earlier))
    return moved + jnp.concatenate([jnp.zeros((HS, HS), F32), later[:, HS:]], axis=1)


def applied(change, state):
    return mm3(halves(change[:, :HS]), halves(state)) + change[:, HS:]


def copy_wait(ref, sem):
    pltpu.make_async_copy(ref, ref, sem).wait()


def layer_kernel(
    q_hbm, k_hbm, v_hbm, gate_hbm, rate_hbm, init_hbm, gain_hbm, plan_hbm, proj_hbm, out_ref,
    q_ref, k_ref, v_ref, gate_ref, rate_ref, init_ref, gain_ref, plan_ref, proj_ref,
    ehi, elo, fd_ref, qh_ref, ql_ref, z0_ref,
    done_first, recv, total, enter, wout, chain, wbuf, normed, prod, sib, rbuf, lbuf, nout, nin, eprod, esib,
    in_sem, fd_send, fd_recv, w_send, w_recv, c_send, c_recv, t_send, t_recv, m_send, m_recv,
    sib_send, sib_recv, r_send, r_recv, l_send, l_recv, n_send, n_recv, e_send, e_recv,
):
    me_c, me_h = lax.axis_index("ctx"), lax.axis_index("head")
    zhi, p = me_c // PLANE, lax.rem(me_c, PLANE)
    x, y = p // SIDE, lax.rem(p, SIDE)
    near, spot = x // 2, lax.rem(p, HALF)
    base = zhi * PLANE + near * HALF
    stage = 2 * zhi + near
    across = zhi * PLANE + lax.rem(p + HALF, PLANE)
    far_across = (1 - zhi) * PLANE + lax.rem(p + HALF, PLANE)
    z, core = me_h // 2, lax.rem(me_h, 2)
    twin = z * 2 + (1 - core)
    partner = (1 - zhi) * PLANE + p
    low, high = z == 0, z == SLOTS - 1
    end = jnp.logical_or(low, high)
    far = SLOTS - 1 - z
    left = (jnp.where(low, partner, me_c), jnp.where(low, 2 * (SLOTS - 1) + core, me_h - 2))
    right = (jnp.where(high, partner, me_c), jnp.where(high, core, me_h + 2))
    seqs, rows = q_ref.shape[0], q_ref.shape[1]
    heads = init_ref.shape[0]
    pairs = seqs * heads
    parts, width = prod.shape[1], prod.shape[-1]

    loads = []
    order = [(k_hbm.at[0], k_ref.at[0]), (v_hbm.at[0], v_ref.at[0]), (gate_hbm, gate_ref), (rate_hbm, rate_ref)]
    order += [(k_hbm.at[1], k_ref.at[1]), (v_hbm.at[1], v_ref.at[1]), (q_hbm, q_ref), (init_hbm, init_ref)]
    order += [(gain_hbm, gain_ref), (plan_hbm, plan_ref), (proj_hbm, proj_ref)]
    for i, (src, dst) in enumerate(order):
        loads.append(pltpu.make_async_copy(src, dst, in_sem.at[i]))
        loads[-1].start()

    barrier = pltpu.get_barrier_semaphore()
    for step in range(1, HALF):
        other = base + lax.rem(spot + step, HALF)
        pl.semaphore_signal(barrier, inc=1, device_id=(other, me_h), device_id_type=MESH)
    for other in ((partner, me_h), (across, me_h), (far_across, me_h), (me_c, twin), left, right):
        pl.semaphore_signal(barrier, inc=1, device_id=other, device_id_type=MESH)

    for i in range(4):
        loads[i].wait()
    etas = []
    for s in range(seqs):
        eta = [gate_ref[s, h : h + 1] * rate_ref[0:1, h : h + 1] for h in range(heads)]
        etas.append(jnp.concatenate(eta + [jnp.zeros((8 - heads, rows), F32)], axis=0).T)

    def home(s, h):
        return (core if s == 0 else 1 - core) * SIDE + h

    def fd_copy(s, h):
        return pltpu.make_async_remote_copy(
            src_ref=fd_ref.at[s * heads + h],
            dst_ref=recv.at[spot],
            send_sem=fd_send.at[s * heads + h],
            recv_sem=fd_recv.at[spot],
            device_id=(base + home(s, h), me_h),
            device_id_type=MESH,
        )

    def make_maps(s):
        for h in range(heads):
            cols = slice(h * HS, (h + 1) * HS)
            k = k_ref[s, :, cols]
            hi, lo = spread(k, v_ref[s, :, cols], etas[s][:, h : h + 1])
            ehi[s * heads + h] = hi
            elo[s * heads + h] = lo
            fd_ref[s * heads + h] = slice_map(k, hi, lo)

    def send_maps(s):
        for i in range(heads):
            h = lax.rem(y + i, heads)
            to = home(s, h)

            @pl.when(to != spot)
            def _():
                fd_copy(s, h).start()

            @pl.when(to == spot)
            def _():
                pltpu.make_async_copy(fd_ref.at[s * heads + h], recv.at[spot], fd_recv.at[spot]).start()

    def readouts(s):
        for h in range(heads):
            j = s * heads + h
            cols = slice(h * HS, (h + 1) * HS)
            qt, z0 = readout(q_ref[s, :, cols], k_ref[s, :, cols], ehi[j], elo[j])
            hi, lo = halves(qt)
            qh_ref[j] = hi
            ql_ref[j] = lo
            z0_ref[j] = z0

    make_maps(0)
    pl.semaphore_wait(barrier, HALF - 1 + 6)
    send_maps(0)
    loads[6].wait()
    readouts(0)
    loads[4].wait()
    loads[5].wait()
    make_maps(1)
    readouts(1)
    for load in loads[7:]:
        load.wait()

    first = lax.rem(x, 2) == core
    mine = jnp.where(first, 0, heads) + y

    def w_copy(c):
        return pltpu.make_async_remote_copy(
            src_ref=wout.at[c],
            dst_ref=wbuf.at[mine],
            send_sem=w_send.at[c],
            recv_sem=w_recv.at[mine],
            device_id=(base + c, me_h),
            device_id_type=MESH,
        )

    def chain_copy(i, to):
        return pltpu.make_async_remote_copy(
            src_ref=chain.at[0],
            dst_ref=chain.at[1],
            send_sem=c_send.at[i],
            recv_sem=c_recv,
            device_id=(to, me_h),
            device_id_type=MESH,
        )

    def map_copy(i, to):
        return pltpu.make_async_remote_copy(
            src_ref=total.at[0],
            dst_ref=total.at[2],
            send_sem=m_send.at[i],
            recv_sem=m_recv,
            device_id=(to, me_h),
            device_id_type=MESH,
        )

    t_copy = pltpu.make_async_remote_copy(
        src_ref=total.at[0],
        dst_ref=total.at[1],
        send_sem=t_send,
        recv_sem=t_recv,
        device_id=(across, me_h),
        device_id_type=MESH,
    )

    def gather_maps(s):
        @pl.when(first if s == 0 else jnp.logical_not(first))
        def _():
            for i in range(SIDE):
                for g in range(2):
                    c = SIDE * g + i
                    copy_wait(recv.at[c], fd_recv.at[c])
                    if i > 0:
                        recv[c] = after(recv[c - 1], recv[c])
            total[0] = after(recv[SIDE - 1], recv[HALF - 1])

            @pl.when(stage == 2)
            def _():
                t_copy.start()

            @pl.when(stage == 0)
            def _():
                enter[0] = init_ref[y]
                chain[0] = applied(total[0], init_ref[y])
                if s == 0:
                    chain_copy(1, far_across).start()
                    chain_copy(2, partner).start()
                chain_copy(0, across).start()

            if s == 0:

                @pl.when(stage == 1)
                def _():
                    map_copy(0, far_across).start()
                    map_copy(1, partner).start()

            for k in range(SIDE, HALF - 1):
                recv[k] = after(recv[SIDE - 1], recv[k])
            if s > 0:

                @pl.when(stage == 1)
                def _():
                    copy_wait(chain.at[1], c_recv)
                    enter[0] = chain[1]
                    chain[0] = applied(total[0], enter[0])
                    chain_copy(0, far_across).start()
                    chain_copy(1, partner).start()

    def give_states(s):
        @pl.when(first if s == 0 else jnp.logical_not(first))
        def _():
            @pl.when(stage > (0 if s == 0 else 1))
            def _():
                copy_wait(chain.at[1], c_recv)
                enter[0] = chain[1]

            if s == 0:

                @pl.when(stage > 1)
                def _():
                    copy_wait(total.at[2], m_recv)
                    enter[0] = applied(total[2], chain[1])

            @pl.when(stage == 3)
            def _():
                t_copy.wait_recv()
                enter[0] = applied(total[1], enter[0])

            wout[0] = enter[0]
            wout[SIDE] = applied(recv[SIDE - 1], enter[0])
            for i in range(2):
                g = lax.rem(x + i, 2)
                for k in range(1, SIDE):
                    wout[SIDE * g + k] = applied(recv[SIDE * g + k - 1], enter[0])
                for i2 in range(SIDE):
                    c = SIDE * g + lax.rem(y + i2, SIDE)

                    @pl.when(c != spot)
                    def _():
                        w_copy(c).start()

                    @pl.when(c == spot)
                    def _():
                        pltpu.make_async_copy(wout.at[c], wbuf.at[mine], w_recv.at[mine]).start()

    def sib_copy(s, q):
        return pltpu.make_async_remote_copy(
            src_ref=prod.at[s, q, 1 - core],
            dst_ref=sib.at[s, q],
            send_sem=sib_send.at[s, q],
            recv_sem=sib_recv.at[s, q],
            device_id=(me_c, twin),
            device_id_type=MESH,
        )

    def line_copy(s, q, b, src, toward_right):
        buf, send, got = (rbuf, r_send, r_recv) if toward_right else (lbuf, l_send, l_recv)
        return pltpu.make_async_remote_copy(
            src_ref=src,
            dst_ref=buf.at[s, q, b],
            send_sem=send.at[s, q, b],
            recv_sem=got.at[s, q, b],
            device_id=right if toward_right else left,
            device_id_type=MESH,
        )

    def own_copy(s, q, b, toward_right):
        return line_copy(s, q, b, prod.at[s, q, core, b], toward_right)

    def far_copy(s, q, toward_right):
        return line_copy(s, q, far, eprod.at[s, q, core], toward_right)

    def rows_copy(s):
        return pltpu.make_async_remote_copy(
            src_ref=nout.at[s],
            dst_ref=nin.at[s],
            send_sem=n_send.at[s],
            recv_sem=n_recv.at[s],
            device_id=(partner, me_h),
            device_id_type=MESH,
        )

    def twin_copy(s, q):
        return pltpu.make_async_remote_copy(
            src_ref=eprod.at[s, q, 1 - core],
            dst_ref=esib.at[s, q],
            send_sem=e_send.at[s, q],
            recv_sem=e_recv.at[s, q],
            device_id=(me_c, twin),
            device_id_type=MESH,
        )

    def each(body):
        lax.fori_loop(0, parts, lambda q, carry: (body(q), carry)[1], 0)

    block = rows // SLOTS
    half = block // 2

    def outputs(s):
        for j in range(s * heads, (s + 1) * heads):
            copy_wait(wbuf.at[j], w_recv.at[j])
        if s == 0:
            send_maps(1)
        for h in range(heads):
            j = s * heads + h
            cols = slice(h * HS, (h + 1) * HS)
            zval = mm3((qh_ref[j], ql_ref[j]), halves(wbuf[j])) + z0_ref[j]
            scale = lax.rsqrt(jnp.mean(zval * zval, axis=-1, keepdims=True) + EPS)
            normed[s, :, cols] = (zval * scale * gain_ref[:, cols]).astype(BF16)

        @pl.when(end)
        def _():
            start = pl.multiple_of(far * block, block)
            nout[s] = normed[s, pl.ds(start, block), :].astype(F32)
            rows_copy(s).start()

        def project(q):
            start = pl.multiple_of(q * width, width)
            part = mm(normed[s], proj_ref[:, pl.ds(start, width)])
            part = part.reshape(SLOTS, 2, half, width)
            prod[s, q, 0] = part[:, 0]
            prod[s, q, 1] = part[:, 1]
            sib_copy(s, q).start()

        def pair_sum(q):
            sib_copy(s, q).wait_recv()
            sib_copy(s, q).wait_send()
            for b in range(SLOTS):
                prod[s, q, core, b] += sib[s, q, b]

            @pl.when(z == 0)
            def _():
                own_copy(s, q, 2, True).start()

            @pl.when(z == 1)
            def _():
                own_copy(s, q, 3, True).start()

            @pl.when(z == 2)
            def _():
                own_copy(s, q, 0, False).start()

            @pl.when(z == 3)
            def _():
                own_copy(s, q, 1, False).start()

        def both(q):
            project(q)
            pair_sum(q - 1)

        project(0)
        lax.fori_loop(1, parts, lambda q, carry: (both(q), carry)[1], 0)
        pair_sum(parts - 1)

    def nearest(s):
        def rightward(q):
            own_copy(s, q, 2, True).wait_send()
            own_copy(s, q, 1, True).start()

        def leftward(q):
            own_copy(s, q, 1, False).wait_send()
            own_copy(s, q, 2, False).start()

        @pl.when(z == 0)
        def _():
            each(rightward)

        @pl.when(z == 3)
        def _():
            each(leftward)

    def far_rows(s):
        @pl.when(end)
        def _():
            copy_wait(nin.at[s], n_recv.at[s])
            there = nin[s].astype(BF16)

            def project(q):
                start = pl.multiple_of(q * width, width)
                part = mm(there, proj_ref[:, pl.ds(start, width)])
                eprod[s, q] = part.reshape(2, half, width)
                twin_copy(s, q).start()

            each(project)

            def pair_sum(q):
                twin_copy(s, q).wait_recv()
                eprod[s, q, core] += esib[s, q]

                @pl.when(low)
                def _():
                    far_copy(s, q, False).start()

                @pl.when(high)
                def _():
                    far_copy(s, q, True).start()

            each(pair_sum)

    def take(s, q, b, buf, got):
        copy_wait(buf.at[s, q, b], got.at[s, q, b])
        prod[s, q, core, b] += buf[s, q, b]

    def forwards(s):
        def up(q):
            take(s, q, 2, rbuf, r_recv)
            own_copy(s, q, 2, True).start()
            take(s, q, 0, lbuf, l_recv)
            own_copy(s, q, 0, False).start()

        def down(q):
            take(s, q, 1, lbuf, l_recv)
            own_copy(s, q, 1, False).start()
            take(s, q, 3, rbuf, r_recv)
            own_copy(s, q, 3, True).start()

        @pl.when(z == 1)
        def _():
            each(up)

        @pl.when(z == 2)
        def _():
            each(down)

    def finals(s):
        for q in range(parts):
            take(s, q, z, rbuf, r_recv)
            take(s, q, z, lbuf, l_recv)
            value = prod[s, q, core, z]
            cols = slice(q * width, (q + 1) * width)
            if s == 0:
                done_first[:, cols] = value
            else:
                other = done_first[:, cols]
                straight = plan_ref[0:1, 0:1] == 0
                out_ref[:, 0, cols] = jnp.where(straight, other, value)
                out_ref[:, 1, cols] = jnp.where(straight, value, other)

    gather_maps(0)
    give_states(0)
    outputs(0)
    far_rows(0)
    gather_maps(1)
    nearest(0)
    forwards(0)
    give_states(1)
    outputs(1)
    far_rows(1)
    nearest(1)
    finals(0)
    forwards(1)
    finals(1)

    def finish(i, carry):
        s, q = i // parts, lax.rem(i, parts)

        @pl.when(z == 0)
        def _():
            own_copy(s, q, 1, True).wait_send()
            far_copy(s, q, False).wait_send()

        @pl.when(z == 1)
        def _():
            own_copy(s, q, 3, True).wait_send()
            own_copy(s, q, 2, True).wait_send()
            own_copy(s, q, 0, False).wait_send()

        @pl.when(z == 2)
        def _():
            own_copy(s, q, 0, False).wait_send()
            own_copy(s, q, 1, False).wait_send()
            own_copy(s, q, 3, True).wait_send()

        @pl.when(z == 3)
        def _():
            own_copy(s, q, 2, False).wait_send()
            far_copy(s, q, True).wait_send()

        @pl.when(end)
        def _():
            twin_copy(s, q).wait_send()

        return carry

    lax.fori_loop(0, seqs * parts, finish, 0)

    @pl.when(end)
    def _():
        for s in range(seqs):
            rows_copy(s).wait_send()

    for j in range(pairs):

        @pl.when(home(j // heads, j % heads) != spot)
        def _():
            fd_copy(j // heads, j % heads).wait_send()

    def done(c, carry):
        @pl.when(c != spot)
        def _():
            w_copy(c).wait_send()

        return carry

    lax.fori_loop(0, HALF, done, 0)

    @pl.when(stage == 0)
    def _():
        chain_copy(0, across).wait_send()

        @pl.when(first)
        def _():
            chain_copy(1, far_across).wait_send()
            chain_copy(2, partner).wait_send()

    @pl.when(jnp.logical_and(stage == 1, first))
    def _():
        map_copy(0, far_across).wait_send()
        map_copy(1, partner).wait_send()

    @pl.when(jnp.logical_and(stage == 1, jnp.logical_not(first)))
    def _():
        chain_copy(0, far_across).wait_send()
        chain_copy(1, partner).wait_send()

    @pl.when(stage == 2)
    def _():
        t_copy.wait_send()


def per_device(queries, keys, values, token_gate, head_rate, init_state, norm_gain, out_proj, plan):
    seqs, rows, width = queries.shape
    heads = init_state.shape[0]
    pairs = seqs * heads
    model = out_proj.shape[1]
    parts = 4
    cols = model // parts
    share = rows // (2 * SLOTS)
    dma = pltpu.SemaphoreType.DMA
    tokens = pltpu.VMEM((seqs, rows, width), BF16)
    line = pltpu.VMEM((seqs, parts, SLOTS, share, cols), F32)
    square = (HS, HS)
    summed = pl.pallas_call(
        layer_kernel,
        out_shape=jax.ShapeDtypeStruct((share, seqs, model), F32),
        in_specs=[pl.BlockSpec(memory_space=pltpu.HBM)] * 9,
        out_specs=pl.BlockSpec(memory_space=pltpu.VMEM),
        scratch_shapes=[
            tokens,
            tokens,
            tokens,
            pltpu.VMEM((seqs, heads, rows), F32),
            pltpu.VMEM((1, heads), F32),
            pltpu.VMEM((heads,) + square, F32),
            pltpu.VMEM((1, width), F32),
            pltpu.VMEM((1, seqs), jnp.int32),
            pltpu.VMEM((width, model), BF16),
            pltpu.VMEM((pairs, rows, 2 * HS), BF16),
            pltpu.VMEM((pairs, rows, 2 * HS), BF16),
            pltpu.VMEM((pairs, HS, 2 * HS), F32),
            pltpu.VMEM((pairs, rows, HS), BF16),
            pltpu.VMEM((pairs, rows, HS), BF16),
            pltpu.VMEM((pairs, rows, HS), F32),
            pltpu.VMEM((share, model), F32),
            pltpu.VMEM((HALF, HS, 2 * HS), F32),
            pltpu.VMEM((3, HS, 2 * HS), F32),
            pltpu.VMEM((2,) + square, F32),
            pltpu.VMEM((HALF,) + square, F32),
            pltpu.VMEM((2,) + square, F32),
            pltpu.VMEM((pairs,) + square, F32),
            tokens,
            pltpu.VMEM((seqs, parts, 2, SLOTS, share, cols), F32),
            line,
            line,
            line,
            pltpu.VMEM((seqs, rows // SLOTS, width), F32),
            pltpu.VMEM((seqs, rows // SLOTS, width), F32),
            pltpu.VMEM((seqs, parts, 2, share, cols), F32),
            pltpu.VMEM((seqs, parts, share, cols), F32),
            dma((11,)),
            dma((pairs,)),
            dma((HALF,)),
            dma((HALF,)),
            dma((pairs,)),
            dma((3,)),
            dma,
            dma,
            dma,
            dma((2,)),
            dma,
            dma((seqs, parts)),
            dma((seqs, parts)),
            dma((seqs, parts, SLOTS)),
            dma((seqs, parts, SLOTS)),
            dma((seqs, parts, SLOTS)),
            dma((seqs, parts, SLOTS)),
            dma((seqs,)),
            dma((seqs,)),
            dma((seqs, parts)),
            dma((seqs, parts)),
        ],
        compiler_params=pltpu.CompilerParams(
            collective_id=0, has_side_effects=True, vmem_limit_bytes=56 * 2**20
        ),
        name="layer",
    )(
        queries,
        keys,
        values,
        token_gate,
        head_rate.reshape(1, heads),
        init_state,
        norm_gain.reshape(1, width),
        plan.reshape(1, seqs),
        out_proj,
    )
    return summed.astype(BF16)


def solution(mesh):
    return jax.shard_map(
        per_device,
        mesh=mesh,
        in_specs=(
            P(None, "ctx", "head"),
            P(None, "ctx", "head"),
            P(None, "ctx", "head"),
            P(None, "head", "ctx"),
            P("head"),
            P("head", None, None),
            P("head"),
            P("head", None),
            P(),
        ),
        out_specs=P(("ctx", "head"), None, None),
        check_vma=False,
    )
```
